32 devices in a mesh: groups: 2 (over x), expert: 16 (over z, y, core).
Axes of the slice: x: 2, y: 2, z: 4, core: 2. Of those that a mesh axis runs over, the one named last changes fastest.
Arguments:
- tokens: bfloat16 [2048, 3072], P(('groups', 'expert')), parts along dimension 0, may hold values from -6 to 6
- cotangent: bfloat16 [2048, 3072], P(('groups', 'expert')), parts along dimension 0, may hold values from -6 to 6
- gate_weights: float32 [2048, 4], P(('groups', 'expert')), parts along dimension 0, may hold values from 0.1 to 1
- expert_ids: int32 [2048, 4], P(('groups', 'expert')), parts along dimension 0, may hold values from 0 to 15, as said below
- w_gate: bfloat16 [3072, 10752], P(None, 'expert'), may hold values from -0.109375 to 0.109375
- w_up: bfloat16 [3072, 10752], P(None, 'expert'), may hold values from -0.109375 to 0.109375
- w_down: bfloat16 [10752, 3072], P('expert'), may hold values from -0.078125 to 0.078125
Outputs:
- input_grad: bfloat16 [2048, 3072], P(('groups', 'expert')), parts along dimension 0
- gate_grad: float32 [2048, 4], P(('groups', 'expert')), parts along dimension 0
The draws below stay inside these ranges and needn't reach their ends.
There are 2 independent parts, one for each index of `groups`. The reference program is written for one: setup_inputs(seed, part) draws one part's arguments, and reference() takes and returns one part's arrays. A program takes and returns all parts, laid end to end along the dimension named above; an argument that names none is the same for every part. Nothing has to cross between parts.
Inputs may be any that keep to these rules, and one draw needn't show every extreme that they name: `expert_ids`: each row names 4 different experts. Within each aligned block of 64 rows no expert below 2 is named by more than 12 rows, and one of them is named by exactly 12 rows.
All inputs are finite; a program needn't handle non-finite values.
Results may differ from the reference program's by a relative error of at most 0.0057.
Values may be sent and summed in bfloat16 or wider, within the bound.
No kernel may reach another device: no remote copies, remote signals or barrier semaphores. Data moves between devices by JAX's collectives and lax.ppermute only.
A program may use at most 128 MiB of HBM per device.

```python
import math
import jax
import jax.numpy as jnp
from jax import lax

D = 3072
EXPERTS = 16
TOP = 4
FFW = 5376
EXP_WIN = 2
TOK_DEV = 64
CAP = 12
SPLIT = 8
UNITS = 672
TOKENS = 1024


def draw_expert_ids(key, part):
    key = jax.random.fold_in(key, 11)
    blocks = TOKENS // TOK_DEV
    count_key, full_key, order_key, other_key, slot_key = jax.random.split(key, 5)
    counts = jax.random.randint(count_key, (blocks, EXP_WIN), CAP // 2, CAP + 1).astype(jnp.int32)
    full_one = jax.random.randint(full_key, (blocks, 1), 0, EXP_WIN).astype(jnp.int32)
    counts = jnp.where(jnp.arange(EXP_WIN, dtype=jnp.int32)[None, :] == full_one, CAP, counts)
    order_keys = jax.random.split(order_key, blocks * EXP_WIN)
    shuffled = jax.vmap(lambda one_key: jax.random.permutation(one_key, TOK_DEV))(order_keys)
    ranks = jnp.argsort(shuffled, axis=1).astype(jnp.int32).reshape(blocks, EXP_WIN, TOK_DEV)
    picked = ranks < counts[:, :, None]
    picked = jnp.transpose(picked, (0, 2, 1)).reshape(TOKENS, EXP_WIN)
    other_keys = jax.random.split(other_key, TOKENS)
    others = jax.vmap(lambda one_key: jax.random.permutation(one_key, EXPERTS - EXP_WIN))(other_keys).astype(jnp.int32) + EXP_WIN
    served_ids = jnp.broadcast_to(jnp.arange(EXP_WIN, dtype=jnp.int32)[None, :], (TOKENS, EXP_WIN))
    candidates = jnp.concatenate((served_ids, others), axis=1).astype(jnp.int32)
    served_score = jnp.where(picked, served_ids, 1000 + served_ids).astype(jnp.int32)
    other_score = jnp.broadcast_to((EXP_WIN + jnp.arange(EXPERTS - EXP_WIN, dtype=jnp.int32))[None, :], (TOKENS, EXPERTS - EXP_WIN))
    scores = jnp.concatenate((served_score, other_score), axis=1)
    order = jnp.argsort(scores, axis=1)[:, :TOP]
    chosen = jnp.take_along_axis(candidates, order, axis=1)
    slot_scores = jax.random.randint(slot_key, (TOKENS, TOP), 0, 1 << 20).astype(jnp.int32) * TOP + jnp.arange(TOP, dtype=jnp.int32)[None, :]
    slot_order = jnp.argsort(slot_scores, axis=1)
    return jnp.take_along_axis(chosen, slot_order, axis=1).astype(jnp.int32)


def steps_of(stream_key, extent, pieces, least, largest):
    def one(dim, blocks):
        draws = jax.random.uniform(jax.random.fold_in(jax.random.fold_in(stream_key, 6), dim), (blocks,), jnp.float32, least / len(pieces), largest / len(pieces))
        return jnp.repeat(jnp.exp(draws), extent[dim] // blocks).reshape((-1,) + (1,) * (len(extent) - dim - 1))

    factor_of = one(*pieces[0])
    for cut in pieces[1:]:
        factor_of = factor_of * one(*cut)
    return factor_of


def scatter_about(own_key, extent, spread, most, cuts=(), kind=jnp.bfloat16):
    loudness = steps_of(own_key, extent, cuts, -0.22, 0.18) if cuts else 1.0
    entries = jax.random.normal(own_key, extent, jnp.float32) * spread * loudness
    return jnp.minimum(jnp.maximum(entries, -most), most).astype(kind)


def setup_inputs(seed: int = 0, part: int = 0) -> dict:
    key_of = jax.random.split(jax.random.key(seed), 8)
    own_keys = jax.random.split(jax.random.fold_in(key_of[7], part), 8)
    return {
        "tokens": scatter_about(own_keys[0], (TOKENS, D), 1.0, 6.0, ((0, 16),)),
        "cotangent": scatter_about(own_keys[1], (TOKENS, D), 1.0, 6.0, ((0, 16),)),
        "gate_weights": jnp.clip(jnp.exp(math.log(1.0) - 2.3025851 * jax.random.uniform(own_keys[2], (TOKENS, TOP), jnp.float32) ** steps_of(own_keys[2], (TOKENS, TOP), ((0, 16),), -0.2, 0.2)), 0.1, 1.0),
        "expert_ids": draw_expert_ids(jax.random.fold_in(jax.random.fold_in(key_of[7], part), 71), part),
        "w_gate": scatter_about(key_of[4], (D, EXP_WIN * FFW), D ** -0.5, 0.109375, ((1, 16),)),
        "w_up": scatter_about(key_of[5], (D, EXP_WIN * FFW), D ** -0.5, 0.109375, ((1, 16),)),
        "w_down": scatter_about(key_of[6], (EXP_WIN * FFW, D), FFW ** -0.5, 0.078125, ((0, 16),)),
    }


def shard_pass(expert_in, expert_grad, w_gate, w_up, w_down):
    gate_pre = jnp.dot(expert_in, w_gate, preferred_element_type=jnp.float32)
    up_proj = jnp.dot(expert_in, w_up, preferred_element_type=jnp.float32)
    sigmoid_gate = jax.nn.sigmoid(gate_pre)
    active = gate_pre * sigmoid_gate
    hidden = (active * up_proj).astype(jnp.bfloat16)
    expert_out = jnp.dot(hidden, w_down, preferred_element_type=jnp.float32)
    gate_score = jnp.sum(expert_grad.astype(jnp.float32) * expert_out, axis=1).astype(jnp.bfloat16)
    hidden_grad = jnp.dot(expert_grad, w_down.T, preferred_element_type=jnp.float32)
    slope = sigmoid_gate * (1.0 + gate_pre * (1.0 - sigmoid_gate))
    gate_back = (hidden_grad * up_proj * slope).astype(jnp.bfloat16)
    up_back = (hidden_grad * active).astype(jnp.bfloat16)
    summed = jnp.dot(gate_back, w_gate.T, preferred_element_type=jnp.float32) + jnp.dot(up_back, w_up.T, preferred_element_type=jnp.float32)
    return summed.astype(jnp.bfloat16), gate_score


def slot_numbers(expert_ids):
    tok_rows = expert_ids.shape[0]
    chosen = expert_ids[:, :, None] == jnp.arange(EXPERTS, dtype=jnp.int32)[None, None, :]
    per_token = jnp.sum(chosen.astype(jnp.float32), axis=1)
    earlier_mask = (jnp.arange(tok_rows)[:, None] > jnp.arange(tok_rows)[None, :]).astype(jnp.float32)
    earlier = jnp.dot(earlier_mask, per_token, preferred_element_type=jnp.float32).astype(jnp.int32)
    return jnp.sum(jnp.where(chosen, earlier[:, None, :], 0), axis=2).astype(jnp.int32)


def reference(tokens, cotangent, gate_weights, expert_ids, w_gate, w_up, w_down):
    blocks = TOKENS // TOK_DEV
    slot_index = jax.vmap(slot_numbers)(expert_ids.reshape(blocks, TOK_DEV, TOP)).reshape(TOKENS, TOP)
    block_of = (jnp.arange(TOKENS, dtype=jnp.int32) // TOK_DEV)[:, None]
    per_expert = blocks * CAP
    total_slots = EXP_WIN * per_expert
    placed = expert_ids * per_expert + block_of * CAP + slot_index
    flat_pos = jnp.where(expert_ids < EXP_WIN, placed, total_slots).reshape(-1).astype(jnp.int32)
    pair_ids = jnp.arange(TOKENS * TOP, dtype=jnp.int32)
    token_of = jnp.full((total_slots,), TOKENS, jnp.int32).at[flat_pos].set(pair_ids // TOP, mode="drop")
    pair_of = jnp.full((total_slots,), TOKENS * TOP, jnp.int32).at[flat_pos].set(pair_ids, mode="drop")
    weight_of = jnp.zeros((total_slots,), jnp.float32).at[flat_pos].set(gate_weights.reshape(-1), mode="drop")
    padded_in = jnp.concatenate((tokens, jnp.zeros((1, D), tokens.dtype)), 0)
    padded_grad = jnp.concatenate((cotangent, jnp.zeros((1, D), cotangent.dtype)), 0)

    def per_expert_step(carry, expert_index):
        grad_sum, scores = carry
        start = (expert_index * per_expert).astype(jnp.int32)
        row_ids = lax.dynamic_slice_in_dim(token_of, start, per_expert)
        pair_here = lax.dynamic_slice_in_dim(pair_of, start, per_expert)
        weight_here = lax.dynamic_slice_in_dim(weight_of, start, per_expert)
        expert_in = padded_in[row_ids]
        expert_grad = padded_grad[row_ids]

        def per_shard(inner, shard_index):
            grad_acc, score_acc = inner
            column_start = (expert_index * FFW + shard_index * UNITS).astype(jnp.int32)
            slot_grad, gate_score = shard_pass(
                expert_in, expert_grad,
                lax.dynamic_slice_in_dim(w_gate, column_start, UNITS, 1),
                lax.dynamic_slice_in_dim(w_up, column_start, UNITS, 1),
                lax.dynamic_slice_in_dim(w_down, column_start, UNITS, 0))
            return (grad_acc + slot_grad.astype(jnp.float32), score_acc + gate_score.astype(jnp.float32)), None

        start_inner = (jnp.zeros((per_expert, D), jnp.float32), jnp.zeros((per_expert,), jnp.float32))
        inner_state, unused = lax.scan(per_shard, start_inner, jnp.arange(SPLIT, dtype=jnp.int32))
        grad_sum = grad_sum.at[row_ids].add(weight_here[:, None] * inner_state[0], mode="drop")
        scores = scores.at[pair_here].set(inner_state[1], mode="drop")
        return (grad_sum, scores), None

    start_state = (jnp.zeros((TOKENS, D), jnp.float32), jnp.zeros((TOKENS * TOP,), jnp.float32))
    final_state, unused = lax.scan(per_expert_step, start_state, jnp.arange(EXP_WIN, dtype=jnp.int32))
    return final_state[0].astype(jnp.bfloat16), final_state[1].reshape(TOKENS, TOP)
```

```python
import functools

import jax
import jax.numpy as jnp
from jax import lax
from jax.experimental import pallas as pl
from jax.experimental.pallas import tpu as pltpu
from jax.sharding import PartitionSpec as P

EXP_WIN = 2
CAP = 12
PAIR = 2 * CAP
LANES = 128
COLS = 512
F32 = jnp.float32
BF16 = jnp.bfloat16
EXACT = lax.Precision.HIGHEST
VMEM = pl.BlockSpec(memory_space=pltpu.VMEM)
SMEM = pl.BlockSpec(memory_space=pltpu.SMEM)


def call(kernel, name, out_shape, in_specs, args, scratch=(), flops=0, limit=16):
    moved = sum(a.size * a.dtype.itemsize for a in args)
    moved += sum(o.size * o.dtype.itemsize for o in out_shape)
    return pl.pallas_call(
        kernel,
        name=name,
        out_shape=out_shape,
        in_specs=in_specs,
        out_specs=[VMEM] * len(out_shape),
        scratch_shapes=list(scratch),
        compiler_params=pltpu.CompilerParams(vmem_limit_bytes=limit << 20),
        cost_estimate=pl.CostEstimate(flops=flops, bytes_accessed=moved, transcendentals=0),
    )(*args)


def struct(shape, dtype):
    return jax.ShapeDtypeStruct(shape, dtype)


def pick_kernel(mine_ref, ids_ref, gates_ref, tok_ref, cot_ref, own_ref, other_ref, place_ref, weight_ref):
    rows = 2 * PAIR
    count = ids_ref.shape[1]
    row = lax.broadcasted_iota(jnp.int32, (rows, count), 0)
    mine = mine_ref[0]
    expert = jnp.where(row < PAIR, mine, EXP_WIN - 1 - mine)
    named = jnp.zeros((rows, count), F32)
    weight = jnp.zeros((rows, count), F32)
    for k in range(ids_ref.shape[0]):
        same = ids_ref[k : k + 1, :] == expert
        named = named + jnp.where(same, 1.0, 0.0)
        weight = weight + jnp.where(same, gates_ref[k : k + 1, :], 0.0)
    before = jnp.where(
        lax.broadcasted_iota(jnp.int32, (count, count), 0)
        < lax.broadcasted_iota(jnp.int32, (count, count), 1),
        1.0,
        0.0,
    )
    slot = jnp.dot(named, before, preferred_element_type=F32)
    taken = sum((row >= CAP * i).astype(jnp.int32) for i in range(1, 4))
    want = (row - CAP * taken).astype(F32)
    place = jnp.where((slot == want) & (named > 0.5), 1.0, 0.0)
    first = (taken == 0) | (taken == 2)
    from_tok = jnp.where(first, place, 0.0).astype(BF16)
    from_cot = jnp.where(first, 0.0, place).astype(BF16)
    picked = jnp.dot(from_tok, tok_ref[...], preferred_element_type=F32)
    picked = picked + jnp.dot(from_cot, cot_ref[...], preferred_element_type=F32)
    own_ref[...] = picked[:PAIR].astype(BF16)
    other_ref[...] = picked[PAIR:].astype(BF16)
    place_ref[...] = place
    weight_ref[...] = place * weight


def nt(a, b):
    return lax.dot_general(a, b, (((1,), (1,)), ((), ())), preferred_element_type=F32)


def shard_kernel(blocks, *refs):
    block_refs = refs[:blocks]
    wg_ref, wu_ref, wd_ref, keep_ref, send_ref, g_ref, u_ref, dh_ref, dg_ref, du_ref = refs[blocks:]
    width = wg_ref.shape[1]
    half = width // 2
    g_ref[...] = jnp.zeros_like(g_ref)
    u_ref[...] = jnp.zeros_like(u_ref)
    dh_ref[...] = jnp.zeros_like(dh_ref)

    def forward(step, carry):
        cols = pl.ds(pl.multiple_of(step * COLS, COLS), COLS)
        parts = [ref[:, cols].astype(F32) for ref in block_refs]
        tok = jnp.concatenate([p[:CAP] for p in parts], axis=0).astype(BF16)
        cot = jnp.concatenate([p[CAP:] for p in parts], axis=0).astype(BF16)
        g_ref[...] += nt(tok, wg_ref[:, cols])
        u_ref[...] += nt(tok, wu_ref[:, cols])
        dh_ref[...] += nt(cot, wd_ref[:, cols])
        return carry

    lax.fori_loop(0, width // COLS, forward, 0)
    g = g_ref[...]
    u = u_ref[...]
    dh = dh_ref[...]
    sig = jax.nn.sigmoid(g)
    act = g * sig
    hidden = (act * u).astype(BF16).astype(F32)
    score = jnp.sum(hidden * dh, axis=1, keepdims=True)
    dg_ref[...] = (dh * u * (sig * (1.0 + g * (1.0 - sig)))).astype(BF16)
    du_ref[...] = (dh * act).astype(BF16)
    rows = keep_ref.shape[0]

    def spread(left, right):
        pieces = []
        for b in range(blocks):
            pieces += [left[CAP * b : CAP * b + CAP], right[CAP * b : CAP * b + CAP]]
        return jnp.concatenate(pieces, axis=0)

    def backward(step, carry):
        halves = []
        for base in (0, half):
            cols = pl.ds(pl.multiple_of(base + step * COLS, COLS), COLS)
            halves.append(
                jnp.dot(dg_ref[...], wg_ref[:, cols], preferred_element_type=F32)
                + jnp.dot(du_ref[...], wu_ref[:, cols], preferred_element_type=F32)
            )
        out = spread(*halves).astype(BF16)
        to = pl.ds(pl.multiple_of(step * COLS, COLS), COLS)
        keep_ref[:, to] = out[:rows]
        send_ref[:, to] = out[rows:]
        return carry

    lax.fori_loop(0, half // COLS, backward, 0)
    score = jnp.broadcast_to(score, (score.shape[0], LANES))
    tail = two_lanes(spread(score, jnp.zeros_like(score))).astype(BF16)
    keep_ref[:, half:] = tail[:rows]
    send_ref[:, half:] = tail[rows:]


def two_lanes(total):
    high = total.astype(BF16).astype(F32)
    lane = lax.broadcasted_iota(jnp.int32, total.shape, 1)
    return jnp.where(lane == 0, high, jnp.where(lane == 1, total - high, 0.0))


def packed(total):
    half = total.shape[1] - LANES
    tail = total[:, half:]
    tail = jnp.broadcast_to(tail[:, 0:1] + tail[:, 1:2], tail.shape)
    return jnp.concatenate([total[:, :half], two_lanes(tail)], axis=1).astype(BF16)


def chip_kernel(keep_ref, got_ref, self_ref, *out_refs):
    total = keep_ref[...].astype(F32) + got_ref[...].astype(F32)
    self_ref[...] = total[:PAIR]
    for i, ref in enumerate(out_refs):
        ref[...] = packed(total[PAIR * (i + 1) : PAIR * (i + 2)])


def total_of(refs):
    total = refs[0][...].astype(F32)
    for ref in refs[1:]:
        total = total + ref[...].astype(F32)
    return total


def other_kernel(*refs):
    refs[-1][...] = packed(total_of(refs[:-1]))


def final_kernel(sources, mine_ref, ids_ref, place_ref, weight_ref, back_ref, *refs):
    own = total_of(refs[:sources])
    grad_ref, gate_ref = refs[sources:]
    other = back_ref[...].astype(F32)
    both = jnp.concatenate([own, other], axis=0)
    half = both.shape[1] - LANES
    rows, count = place_ref.shape
    eye = jnp.where(
        lax.broadcasted_iota(jnp.int32, (count, count), 0)
        == lax.broadcasted_iota(jnp.int32, (count, count), 1),
        1.0,
        0.0,
    )
    weight = lax.dot_general(
        eye, weight_ref[...], (((1,), (1,)), ((), ())), precision=EXACT, preferred_element_type=F32
    )
    lane = lax.broadcasted_iota(jnp.int32, weight.shape, 1)
    first = (lane < CAP) | ((lane >= PAIR) & (lane < PAIR + CAP))
    for i in range(2):
        part = jnp.where(first == (i == 0), weight, 0.0)
        out = jnp.dot(part, both[:, :half], precision=EXACT, preferred_element_type=F32)
        grad_ref[:, half * i : half * (i + 1)] = out.astype(BF16)
    tail = both[:, half:]
    score = (tail[:, 0:1] + tail[:, 1:2]) * place_ref[...]
    mine = mine_ref[0]
    ids = ids_ref[...]
    own_score = jnp.sum(score[:PAIR], axis=0, keepdims=True)
    other_score = jnp.sum(score[PAIR:], axis=0, keepdims=True)
    gate_ref[...] = jnp.where(ids == mine, own_score, 0.0) + jnp.where(
        ids == EXP_WIN - 1 - mine, other_score, 0.0
    )


def per_device(tokens, cotangent, gate_weights, expert_ids, w_gate, w_up, w_down):
    devices = lax.axis_size("expert")
    split = devices // EXP_WIN
    evens = range(2, split, 2)
    width = tokens.shape[1]
    units = w_down.shape[0]
    count = tokens.shape[0]
    wide = width // 2 + LANES
    mine = (lax.axis_index("expert") // split).astype(jnp.int32).reshape(1)
    ids = expert_ids.T
    gates = gate_weights.T
    weights = (w_gate.T, w_up.T, w_down)

    def swap(x, offset):
        return lax.ppermute(x, "expert", [(i, i ^ offset) for i in range(devices)])

    own, other, place, weight = call(
        pick_kernel,
        "pick",
        [struct((PAIR, width), BF16)] * 2 + [struct((2 * PAIR, count), F32)] * 2,
        [SMEM] + [VMEM] * 4,
        (mine, ids, gates, tokens, cotangent),
        flops=4 * 2 * PAIR * count * width,
    )

    def spread_rows(block):
        return [block] + [swap(block, k) for k in evens]

    def shard(blocks):
        blocks = blocks + [swap(b, 1) for b in blocks]
        m = len(blocks) * CAP
        return call(
            functools.partial(shard_kernel, len(blocks)),
            "shard",
            [struct((m, wide), BF16)] * 2,
            [VMEM] * (len(blocks) + 3),
            (*blocks, *weights),
            [pltpu.VMEM((m, units), F32)] * 3 + [pltpu.VMEM((m, units), BF16)] * 2,
            flops=10 * m * width * units,
        )

    def chip_sums(keep, send):
        got = swap(send, 1)
        return call(
            chip_kernel,
            "chip",
            [struct((PAIR, wide), F32)] + [struct((PAIR, wide), BF16)] * len(evens),
            [VMEM] * 2,
            (keep, got),
        )

    def returned(sums):
        return [sums[0]] + [swap(s, k) for s, k in zip(sums[1:], evens)]

    crossed = swap(other, split)
    own_blocks = spread_rows(own)
    cross_blocks = spread_rows(crossed)
    own_back = returned(chip_sums(*shard(own_blocks)))
    cross_back = returned(chip_sums(*shard(cross_blocks)))
    (cross_total,) = call(
        other_kernel, "other", [struct((PAIR, wide), BF16)], [VMEM] * len(cross_back), tuple(cross_back)
    )
    back = swap(cross_total, split)
    grad, gate_grad = call(
        functools.partial(final_kernel, len(own_back)),
        "final",
        [struct((count, width), BF16), struct(ids.shape, F32)],
        [SMEM] + [VMEM] * (4 + len(own_back)),
        (mine, ids, place, weight, back, *own_back),
    )
    return (grad, gate_grad.T)


def solution(mesh):
    rows = P(("groups", "expert"), None)
    return jax.shard_map(
        per_device,
        mesh=mesh,
        in_specs=(rows, rows, rows, rows, P(None, "expert"), P(None, "expert"), P("expert", None)),
        out_specs=(rows, rows),
        check_vma=False,
    )
```

```python
import functools

import jax
import jax.numpy as jnp
from jax import lax
from jax.experimental import pallas as pl
from jax.experimental.pallas import tpu as pltpu
from jax.sharding import PartitionSpec as P

EXP_WIN = 2
CAP = 12
PAIR = 2 * CAP
LANES = 128
ROWS = 16
SKIP = CAP - (PAIR - ROWS)
F32 = jnp.float32
BF16 = jnp.bfloat16
PICK_LIMIT = 60
GATE_FLOPS = 10**10
VMEM = pl.BlockSpec(memory_space=pltpu.VMEM)
HBM = pl.BlockSpec(memory_space=pltpu.HBM)
SMEM = pl.BlockSpec(memory_space=pltpu.SMEM)


def call(kernel, name, out_shape, in_specs, args, scratch=(), flops=0, limit=16):
    moved = sum(a.size * a.dtype.itemsize for a in args)
    moved += sum(o.size * o.dtype.itemsize for o in out_shape)
    return pl.pallas_call(
        kernel,
        name=name,
        out_shape=out_shape,
        in_specs=in_specs,
        out_specs=[VMEM] * len(out_shape),
        scratch_shapes=list(scratch),
        compiler_params=pltpu.CompilerParams(vmem_limit_bytes=limit << 20),
        cost_estimate=pl.CostEstimate(flops=flops, bytes_accessed=moved, transcendentals=0),
    )(*args)


def struct(shape, dtype):
    return jax.ShapeDtypeStruct(shape, dtype)


def pick_kernel(mine_ref, ids_hbm, gates_hbm, tok_hbm, cot_hbm, own_ref, other_ref, ids_ref, place_ref, weight_ref, gates_ref, tok_ref, cot_ref, sems):
    pairs = ((ids_hbm, ids_ref), (gates_hbm, gates_ref), (tok_hbm, tok_ref), (cot_hbm, cot_ref))
    copies = [pltpu.make_async_copy(a, b, sems.at[i]) for i, (a, b) in enumerate(pairs)]
    for copy in copies:
        copy.start()
    rows = 2 * PAIR
    count = ids_ref.shape[1]
    row = lax.broadcasted_iota(jnp.int32, (rows, count), 0)
    mine = mine_ref[0]
    expert = jnp.where(row < PAIR, mine, EXP_WIN - 1 - mine)
    before = jnp.where(
        lax.broadcasted_iota(jnp.int32, (count, count), 0)
        < lax.broadcasted_iota(jnp.int32, (count, count), 1),
        1.0,
        0.0,
    )
    taken = sum((row >= CAP * i).astype(jnp.int32) for i in range(1, 4))
    want = (row - CAP * taken).astype(F32)
    first = (taken == 0) | (taken == 2)
    named = jnp.zeros((rows, count), F32)
    weight = jnp.zeros((rows, count), F32)
    copies[0].wait()
    copies[1].wait()
    for k in range(ids_ref.shape[0]):
        same = ids_ref[k : k + 1, :] == expert
        named = named + jnp.where(same, 1.0, 0.0)
        weight = weight + jnp.where(same, gates_ref[k : k + 1, :], 0.0)
    slot = jnp.dot(named, before, preferred_element_type=F32)
    place = jnp.where((slot == want) & (named > 0.5), 1.0, 0.0)
    upper = jnp.where(first, place, 0.0).astype(BF16)
    lower = jnp.where(first, 0.0, place).astype(BF16)
    copies[2].wait()
    copies[3].wait()

    def rows_of(part, a, b):
        picked = jnp.dot(upper[part], a, preferred_element_type=F32)
        return (picked + jnp.dot(lower[part], b, preferred_element_type=F32)).astype(BF16)

    half = tok_ref.shape[1] // 2
    for i, ref in enumerate((tok_ref, cot_ref)):
        other_ref[PAIR * i : PAIR * (i + 1), :] = rows_of(slice(PAIR, rows), ref[:, :half], ref[:, half:])
    own_ref[...] = rows_of(slice(0, PAIR), tok_ref[...], cot_ref[...])
    place_ref[...] = place
    weight_ref[...] = place * weight


def split_two(x):
    high = x.astype(BF16).astype(F32)
    return high, x - high


def layout_kernel(weight_ref, left_ref, right_ref):
    weight = weight_ref[...]
    own_high, own_low = split_two(weight[:PAIR])
    other_high, other_low = split_two(weight[PAIR:])
    rest = jnp.zeros((LANES - 5 * PAIR, weight.shape[1]), F32)
    table = jnp.concatenate([other_high, other_low, own_high, own_low, own_high, rest], axis=0)
    row = lax.broadcasted_iota(jnp.int32, table.shape, 0)
    block = sum((row >= PAIR * i).astype(jnp.int32) for i in range(1, 6))
    first = row - PAIR * block < CAP
    left_ref[...] = jnp.where(first, table, 0.0).T.astype(BF16)
    right_ref[...] = jnp.where(first, 0.0, table).T.astype(BF16)


def gate_kernel(*refs):
    refs[-1][...] = jnp.zeros_like(refs[-1])


def nt(a, b):
    return lax.dot_general(a, b, (((1,), (1,)), ((), ())), preferred_element_type=F32)


def tn(a, b):
    return lax.dot_general(a, b, (((0,), (0,)), ((), ())), preferred_element_type=F32)


def weave(left, right, blocks):
    low = lax.broadcasted_iota(jnp.int32, (8, left.shape[1]), 0) < SKIP
    pieces = []
    for b in range(blocks):
        a = ROWS * b
        pieces += [
            left[a : a + 8],
            jnp.where(low, left[a + 8 : a + ROWS], right[a : a + 8]),
            right[a + 8 : a + ROWS],
        ]
    return jnp.concatenate(pieces, axis=0)


def halves(own_refs, own_at, other_refs, other_at, left_ref, right_ref):
    half = left_ref.shape[1]
    upper = slice(other_at, other_at + ROWS)
    lower = slice(other_at + PAIR - ROWS, other_at + PAIR)
    for b, ref in enumerate(own_refs):
        rows = slice(ROWS * b, ROWS * (b + 1))
        left_ref[rows, :] = ref[own_at, :half]
        right_ref[rows, :] = ref[own_at, half:]
    for b, ref in enumerate(other_refs, len(own_refs)):
        rows = slice(ROWS * b, ROWS * (b + 1))
        left_ref[rows, :] = ref[upper, :]
        right_ref[rows, :] = ref[lower, :]


def back_by(x):
    return pltpu.roll(x, x.shape[1] - SKIP, 1)


def forward_kernel(blocks, *refs):
    own_refs, other_refs = refs[:blocks], refs[blocks : 2 * blocks]
    wg_ref, wu_ref, _, slope_ref, active_ref, hidden_ref, left_ref, right_ref = refs[2 * blocks :]
    half = left_ref.shape[1]
    halves(own_refs, slice(0, ROWS), other_refs, 0, left_ref, right_ref)
    split = ROWS * blocks

    def product(w_ref):
        a = nt(w_ref[:, :half], left_ref[...])
        b = nt(w_ref[:, half:], right_ref[...])
        return a + jnp.concatenate([b[:, :split], back_by(b[:, split:])], axis=1)

    g = product(wg_ref)
    u = product(wu_ref)
    sig = jax.nn.sigmoid(g)
    act = g * sig
    hidden_ref[...] = (act * u).astype(BF16)
    active_ref[...] = act
    slope_ref[...] = u * (sig * (1.0 + g * (1.0 - sig)))


def backward_kernel(blocks, *refs):
    own_refs, other_refs = refs[:blocks], refs[blocks : 2 * blocks]
    slope_ref, active_ref, hidden_ref, wg_ref, wu_ref, wd_ref = refs[2 * blocks : 2 * blocks + 6]
    keep_ref, send_ref, left_ref, right_ref = refs[2 * blocks + 6 :]
    half = left_ref.shape[1]
    halves(own_refs, slice(PAIR - ROWS, PAIR), other_refs, PAIR, left_ref, right_ref)
    split = ROWS * blocks
    a = nt(wd_ref[:, :half], left_ref[...])
    b = nt(wd_ref[:, half:], right_ref[...])
    own = back_by(a[:, :split] + b[:, :split])
    dh = jnp.concatenate([own, a[:, split:] + back_by(b[:, split:])], axis=1)
    score = jnp.sum(hidden_ref[...].astype(F32) * dh, axis=0, keepdims=True)
    grads = (dh * slope_ref[...], dh * active_ref[...])

    def put(to, left, right):
        for i in range(2):
            mine = slice(split * i, split * i + split // 2)
            theirs = slice(split * i + split // 2, split * (i + 1))
            rows = slice(PAIR * blocks // 2 * i, PAIR * blocks // 2 * (i + 1))
            keep_ref[rows, to] = weave(left[mine], right[mine], blocks // 2).astype(BF16)
            send_ref[rows, to] = weave(left[theirs], right[theirs], blocks // 2).astype(BF16)

    def back(pair, cols):
        return jnp.dot(pair[0], wg_ref[:, cols], preferred_element_type=F32) + jnp.dot(
            pair[1], wu_ref[:, cols], preferred_element_type=F32
        )

    upper = [x.T.astype(BF16) for x in grads]
    lower = [pltpu.roll(x, SKIP, 1).T.astype(BF16) for x in grads]
    put(slice(0, half), back(upper, slice(0, half)), back(lower, slice(half, 2 * half)))
    score = two_lanes(jnp.broadcast_to(score, (LANES, 2 * split)).T)
    put(slice(half, half + LANES), score, jnp.zeros_like(score))


def two_lanes(total):
    high, low = split_two(total)
    lane = lax.broadcasted_iota(jnp.int32, total.shape, 1)
    return jnp.where(lane == 0, high, jnp.where(lane == 1, low, 0.0))


def packed(total):
    half = total.shape[1] - LANES
    tail = total[:, half:]
    tail = jnp.broadcast_to(tail[:, 0:1] + tail[:, 1:2], tail.shape)
    return jnp.concatenate([total[:, :half], two_lanes(tail)], axis=1).astype(BF16)


def chip_kernel(keep_ref, got_ref, *out_refs):
    total = keep_ref[...].astype(F32) + got_ref[...].astype(F32)
    for i, ref in enumerate(out_refs):
        part = total[PAIR * i : PAIR * (i + 1)]
        ref[...] = part if ref.dtype == F32 else packed(part)


def total_of(refs):
    total = refs[0][...].astype(F32)
    for ref in refs[1:]:
        total = total + ref[...].astype(F32)
    return total


def other_kernel(*refs):
    refs[-1][...] = packed(total_of(refs[:-1]))


def final_kernel(sources, mine_ref, ids_ref, place_ref, left_ref, right_ref, back_ref, *refs):
    own = total_of(refs[:sources])
    grad_ref, gate_ref = refs[sources:]
    back = back_ref[...]
    half = own.shape[1] - LANES
    own_high, own_low = split_two(own[:, :half])
    other = back[:, :half].astype(F32)
    rest = jnp.zeros((LANES - 5 * PAIR, half), F32)
    table = jnp.concatenate([other, other, own_high, own_high, own_low, rest], axis=0).astype(BF16)
    for i, ref in enumerate((left_ref, right_ref)):
        out = jnp.dot(ref[...], table, preferred_element_type=F32)
        grad_ref[:, half * i : half * (i + 1)] = out.astype(BF16)
    tail = jnp.concatenate([own[:, half:], back[:, half:].astype(F32)], axis=0)
    score = (tail[:, 0:1] + tail[:, 1:2]) * place_ref[...]
    mine = mine_ref[0]
    ids = ids_ref[...]
    own_score = jnp.sum(score[:PAIR], axis=0, keepdims=True)
    other_score = jnp.sum(score[PAIR:], axis=0, keepdims=True)
    gate_ref[...] = jnp.where(ids == mine, own_score, 0.0) + jnp.where(
        ids == EXP_WIN - 1 - mine, other_score, 0.0
    )


def per_device(tokens, cotangent, gate_weights, expert_ids, w_gate, w_up, w_down):
    devices = lax.axis_size("expert")
    split = devices // EXP_WIN
    evens = range(2, split, 2)
    width = tokens.shape[1]
    units = w_down.shape[0]
    count = tokens.shape[0]
    wide = width // 2 + LANES
    mine = (lax.axis_index("expert") // split).astype(jnp.int32).reshape(1)
    ids = expert_ids.T
    gates = gate_weights.T

    def swap(x, offset):
        return lax.ppermute(x, "expert", [(i, i ^ offset) for i in range(devices)])

    def like(x):
        return pltpu.VMEM(x.shape, x.dtype)

    own, other, ids, place, weight = call(
        pick_kernel,
        "pick",
        [struct((PAIR, width), BF16), struct((2 * PAIR, width // 2), BF16)]
        + [struct(ids.shape, ids.dtype)]
        + [struct((2 * PAIR, count), F32)] * 2,
        [SMEM] + [HBM] * 4,
        (mine, ids, gates, tokens, cotangent),
        [like(gates), like(tokens), like(cotangent), pltpu.SemaphoreType.DMA((4,))],
        flops=4 * 2 * PAIR * count * width,
        limit=PICK_LIMIT,
    )
    weights = (w_gate.T, w_up.T, w_down)
    left, right = call(
        layout_kernel,
        "layout",
        [struct((count, LANES), BF16)] * 2,
        [VMEM],
        (weight,),
    )

    def near(block):
        return [block] + [swap(block, k) for k in evens]

    def both_cores(blocks):
        return blocks + [swap(b, 1) for b in blocks]

    rows = 2 * split * ROWS
    stacked = [pltpu.VMEM((rows, width // 2), BF16)] * 2
    def gate(*args):
        return call(
            gate_kernel, "gate", [struct((8, LANES), F32)], [VMEM] * len(args), args, flops=GATE_FLOPS
        )[0]

    together = lax.optimization_barrier
    other = swap(other, split)
    own, token = together((own, gate()))
    other, token = together((other, token))
    own = near(own)
    other = near(other)
    own, other[-1] = together((own, other[-1]))
    own = both_cores(own)
    other = both_cores(other)
    states = call(
        functools.partial(forward_kernel, split),
        "forward",
        [struct((units, rows), F32)] * 2 + [struct((units, rows), BF16)],
        [VMEM] * (2 * split + 3),
        (*own, *other, *weights[:2], token),
        stacked,
        flops=4 * rows * width * units,
        limit=24,
    )
    keep, send = call(
        functools.partial(backward_kernel, split),
        "backward",
        [struct((PAIR * split, wide), BF16)] * 2,
        [VMEM] * (2 * split + 6),
        (*own, *other, *states, *weights),
        stacked,
        flops=6 * rows * width * units,
        limit=24,
    )
    got = swap(send, 1)
    kinds = [struct((PAIR, wide), F32)] + [struct((PAIR, wide), BF16)] * len(evens)
    sums = call(chip_kernel, "chip", kinds * 2, [VMEM] * 2, (keep, got))

    def returned(sums):
        return [sums[0]] + [swap(s, k) for s, k in zip(sums[1:], evens)]

    cross_back = returned(sums[len(kinds) :])
    own_back = returned(sums[: len(kinds)])
    (cross_total,) = call(
        other_kernel, "other", [struct((PAIR, wide), BF16)], [VMEM] * len(cross_back), tuple(cross_back)
    )
    back = swap(cross_total, split)
    grad, gate_grad = call(
        functools.partial(final_kernel, len(own_back)),
        "final",
        [struct((count, width), BF16), struct(ids.shape, F32)],
        [SMEM] + [VMEM] * (5 + len(own_back)),
        (mine, ids, place, left, right, back, *own_back),
    )
    return (grad, gate_grad.T)


def solution(mesh):
    rows = P(("groups", "expert"), None)
    return jax.shard_map(
        per_device,
        mesh=mesh,
        in_specs=(rows, rows, rows, rows, P(None, "expert"), P(None, "expert"), P("expert", None)),
        out_specs=(rows, rows),
        check_vma=False,
    )
```

```python
import functools

import jax
import jax.numpy as jnp
from jax import lax
from jax.experimental import pallas as pl
from jax.experimental.pallas import tpu as pltpu
from jax.sharding import PartitionSpec as P

EXP_WIN = 2
CAP = 12
PAIR = 2 * CAP
LANES = 128
ROWS = 16
SKIP = CAP - (PAIR - ROWS)
F32 = jnp.float32
BF16 = jnp.bfloat16
PICK_LIMIT = 60
GATE_FLOPS = 10**10
VMEM = pl.BlockSpec(memory_space=pltpu.VMEM)
HBM = pl.BlockSpec(memory_space=pltpu.HBM)
SMEM = pl.BlockSpec(memory_space=pltpu.SMEM)


def call(kernel, name, out_shape, in_specs, args, scratch=(), flops=0, limit=16):
    moved = sum(a.size * a.dtype.itemsize for a in args)
    moved += sum(o.size * o.dtype.itemsize for o in out_shape)
    return pl.pallas_call(
        kernel,
        name=name,
        out_shape=out_shape,
        in_specs=in_specs,
        out_specs=[VMEM] * len(out_shape),
        scratch_shapes=list(scratch),
        compiler_params=pltpu.CompilerParams(vmem_limit_bytes=limit << 20),
        cost_estimate=pl.CostEstimate(flops=flops, bytes_accessed=moved, transcendentals=0),
    )(*args)


def struct(shape, dtype):
    return jax.ShapeDtypeStruct(shape, dtype)


def pick_kernel(mine_ref, ids_hbm, gates_hbm, tok_hbm, cot_hbm, own_ref, other_ref, ids_ref, place_ref, weight_ref, gates_ref, tok_ref, cot_ref, sems):
    pairs = ((ids_hbm, ids_ref), (gates_hbm, gates_ref), (tok_hbm, tok_ref), (cot_hbm, cot_ref))
    copies = [pltpu.make_async_copy(a, b, sems.at[i]) for i, (a, b) in enumerate(pairs)]
    for copy in copies:
        copy.start()
    rows = 2 * PAIR
    count = ids_ref.shape[1]
    row = lax.broadcasted_iota(jnp.int32, (rows, count), 0)
    mine = mine_ref[0]
    expert = jnp.where(row < PAIR, mine, EXP_WIN - 1 - mine)
    before = jnp.where(
        lax.broadcasted_iota(jnp.int32, (count, count), 0)
        < lax.broadcasted_iota(jnp.int32, (count, count), 1),
        1.0,
        0.0,
    )
    taken = sum((row >= CAP * i).astype(jnp.int32) for i in range(1, 4))
    want = (row - CAP * taken).astype(F32)
    first = (taken == 0) | (taken == 2)
    named = jnp.zeros((rows, count), F32)
    weight = jnp.zeros((rows, count), F32)
    copies[0].wait()
    copies[1].wait()
    for k in range(ids_ref.shape[0]):
        same = ids_ref[k : k + 1, :] == expert
        named = named + jnp.where(same, 1.0, 0.0)
        weight = weight + jnp.where(same, gates_ref[k : k + 1, :], 0.0)
    slot = jnp.dot(named, before, preferred_element_type=F32)
    place = jnp.where((slot == want) & (named > 0.5), 1.0, 0.0)
    upper = jnp.where(first, place, 0.0).astype(BF16)
    lower = jnp.where(first, 0.0, place).astype(BF16)
    copies[2].wait()
    copies[3].wait()

    def rows_of(part, a, b):
        picked = jnp.dot(upper[part], a, preferred_element_type=F32)
        return (picked + jnp.dot(lower[part], b, preferred_element_type=F32)).astype(BF16)

    half = tok_ref.shape[1] // 2
    for i, ref in enumerate((tok_ref, cot_ref)):
        other_ref[PAIR * i : PAIR * (i + 1), :] = rows_of(slice(PAIR, rows), ref[:, :half], ref[:, half:])
    own_ref[...] = rows_of(slice(0, PAIR), tok_ref[...], cot_ref[...])
    place_ref[...] = place
    weight_ref[...] = place * weight


def split_two(x):
    high = x.astype(BF16).astype(F32)
    return high, x - high


def layout_kernel(weight_ref, *out_refs):
    weight = weight_ref[...]
    for i, (part, lows) in enumerate(((weight[:PAIR], 1), (weight[PAIR:], 0))):
        high, low = split_two(part)
        parts = [high, low] + [high] * lows
        rest = jnp.zeros((LANES - PAIR * len(parts), weight.shape[1]), F32)
        table = jnp.concatenate([*parts, rest], axis=0)
        row = lax.broadcasted_iota(jnp.int32, table.shape, 0)
        block = sum((row >= PAIR * j).astype(jnp.int32) for j in range(1, len(parts) + 1))
        first = row - PAIR * block < CAP
        out_refs[2 * i][...] = jnp.where(first, table, 0.0).T.astype(BF16)
        out_refs[2 * i + 1][...] = jnp.where(first, 0.0, table).T.astype(BF16)


def gate_kernel(*refs):
    refs[-1][...] = jnp.zeros_like(refs[-1])


def nt(a, b):
    return lax.dot_general(a, b, (((1,), (1,)), ((), ())), preferred_element_type=F32)


def tn(a, b):
    return lax.dot_general(a, b, (((0,), (0,)), ((), ())), preferred_element_type=F32)


def weave(left, right, blocks):
    low = lax.broadcasted_iota(jnp.int32, (8, left.shape[1]), 0) < SKIP
    pieces = []
    for b in range(blocks):
        a = ROWS * b
        pieces += [
            left[a : a + 8],
            jnp.where(low, left[a + 8 : a + ROWS], right[a : a + 8]),
            right[a + 8 : a + ROWS],
        ]
    return jnp.concatenate(pieces, axis=0)


def halves(own_refs, own_at, other_refs, other_at, left_ref, right_ref):
    half = left_ref.shape[1]
    upper = slice(other_at, other_at + ROWS)
    lower = slice(other_at + PAIR - ROWS, other_at + PAIR)
    for b, ref in enumerate(own_refs):
        rows = slice(ROWS * b, ROWS * (b + 1))
        left_ref[rows, :] = ref[own_at, :half]
        right_ref[rows, :] = ref[own_at, half:]
    for b, ref in enumerate(other_refs, len(own_refs)):
        rows = slice(ROWS * b, ROWS * (b + 1))
        left_ref[rows, :] = ref[upper, :]
        right_ref[rows, :] = ref[lower, :]


def back_by(x):
    return pltpu.roll(x, x.shape[1] - SKIP, 1)


def forward_kernel(blocks, *refs):
    own_refs, other_refs = refs[:blocks], refs[blocks : 2 * blocks]
    wg_ref, wu_ref, _, slope_ref, active_ref, hidden_ref, left_ref, right_ref = refs[2 * blocks :]
    half = left_ref.shape[1]
    halves(own_refs, slice(0, ROWS), other_refs, 0, left_ref, right_ref)
    split = ROWS * blocks

    def product(w_ref):
        a = nt(w_ref[:, :half], left_ref[...])
        b = nt(w_ref[:, half:], right_ref[...])
        return a + jnp.concatenate([b[:, :split], back_by(b[:, split:])], axis=1)

    g = product(wg_ref)
    u = product(wu_ref)
    sig = jax.nn.sigmoid(g)
    act = g * sig
    hidden_ref[...] = (act * u).astype(BF16)
    active_ref[...] = act
    slope_ref[...] = u * (sig * (1.0 + g * (1.0 - sig)))


def backward_kernel(blocks, *refs):
    own_refs, other_refs = refs[:blocks], refs[blocks : 2 * blocks]
    slope_ref, active_ref, hidden_ref, wg_ref, wu_ref, wd_ref = refs[2 * blocks : 2 * blocks + 6]
    out_refs, left_ref, right_ref = refs[2 * blocks + 6 : -2], *refs[-2:]
    half = left_ref.shape[1]
    halves(own_refs, slice(PAIR - ROWS, PAIR), other_refs, PAIR, left_ref, right_ref)
    split = ROWS * blocks
    a = nt(wd_ref[:, :half], left_ref[...])
    b = nt(wd_ref[:, half:], right_ref[...])
    own = back_by(a[:, :split] + b[:, :split])
    dh = jnp.concatenate([own, a[:, split:] + back_by(b[:, split:])], axis=1)
    score = jnp.sum(hidden_ref[...].astype(F32) * dh, axis=0, keepdims=True)
    grads = (dh * slope_ref[...], dh * active_ref[...])

    def put(to, left, right):
        for i, ref in enumerate(out_refs):
            part = slice(split // 2 * i, split // 2 * (i + 1))
            ref[:, to] = weave(left[part], right[part], blocks // 2).astype(BF16)

    def back(pair, cols):
        return jnp.dot(pair[0], wg_ref[:, cols], preferred_element_type=F32) + jnp.dot(
            pair[1], wu_ref[:, cols], preferred_element_type=F32
        )

    upper = [x.T.astype(BF16) for x in grads]
    lower = [pltpu.roll(x, SKIP, 1).T.astype(BF16) for x in grads]
    put(slice(0, half), back(upper, slice(0, half)), back(lower, slice(half, 2 * half)))
    score = two_lanes(jnp.broadcast_to(score, (LANES, 2 * split)).T)
    put(slice(half, half + LANES), score, jnp.zeros_like(score))


def two_lanes(total):
    high, low = split_two(total)
    lane = lax.broadcasted_iota(jnp.int32, total.shape, 1)
    return jnp.where(lane == 0, high, jnp.where(lane == 1, low, 0.0))


def packed(total):
    half = total.shape[1] - LANES
    tail = total[:, half:]
    tail = jnp.broadcast_to(tail[:, 0:1] + tail[:, 1:2], tail.shape)
    return jnp.concatenate([total[:, :half], two_lanes(tail)], axis=1).astype(BF16)


def chip_kernel(keep_ref, got_ref, *out_refs):
    total = keep_ref[...].astype(F32) + got_ref[...].astype(F32)
    for i, ref in enumerate(out_refs):
        part = total[PAIR * i : PAIR * (i + 1)]
        ref[...] = part if ref.dtype == F32 else packed(part)


def total_of(refs):
    total = refs[0][...].astype(F32)
    for ref in refs[1:]:
        total = total + ref[...].astype(F32)
    return total


def other_kernel(*refs):
    refs[-1][...] = packed(total_of(refs[:-1]))


def weighted(tables, parts):
    rest = jnp.zeros((LANES - PAIR * len(parts), parts[0].shape[1]), F32)
    rows = jnp.concatenate([*parts, rest], axis=0).astype(BF16)
    return [jnp.dot(ref[...], rows, preferred_element_type=F32) for ref in tables]


def own_kernel(left_ref, right_ref, *refs):
    grad_ref, tail_ref = refs[-2:]
    own = total_of(refs[:-2])
    half = own.shape[1] - LANES
    high, low = split_two(own[:, :half])
    for i, out in enumerate(weighted((left_ref, right_ref), (high, high, low))):
        grad_ref[:, half * i : half * (i + 1)] = out
    tail_ref[...] = own[:, half:]


def final_kernel(mine_ref, ids_ref, place_ref, left_ref, right_ref, own_ref, tail_ref, back_ref, grad_ref, gate_ref):
    back = back_ref[...].astype(F32)
    half = back.shape[1] - LANES
    other = back[:, :half]
    for i, out in enumerate(weighted((left_ref, right_ref), (other, other))):
        cols = slice(half * i, half * (i + 1))
        grad_ref[:, cols] = (own_ref[:, cols] + out).astype(BF16)
    tail = jnp.concatenate([tail_ref[...], back[:, half:]], axis=0)
    score = (tail[:, 0:1] + tail[:, 1:2]) * place_ref[...]
    mine = mine_ref[0]
    ids = ids_ref[...]
    own_score = jnp.sum(score[:PAIR], axis=0, keepdims=True)
    other_score = jnp.sum(score[PAIR:], axis=0, keepdims=True)
    gate_ref[...] = jnp.where(ids == mine, own_score, 0.0) + jnp.where(
        ids == EXP_WIN - 1 - mine, other_score, 0.0
    )


def per_device(tokens, cotangent, gate_weights, expert_ids, w_gate, w_up, w_down):
    devices = lax.axis_size("expert")
    split = devices // EXP_WIN
    evens = list(range(split - 2, 0, -2))
    width = tokens.shape[1]
    units = w_down.shape[0]
    count = tokens.shape[0]
    wide = width // 2 + LANES
    mine = (lax.axis_index("expert") // split).astype(jnp.int32).reshape(1)
    ids = expert_ids.T
    gates = gate_weights.T

    def swap(x, offset):
        return lax.ppermute(x, "expert", [(i, i ^ offset) for i in range(devices)])

    def like(x):
        return pltpu.VMEM(x.shape, x.dtype)

    own, other, ids, place, weight = call(
        pick_kernel,
        "pick",
        [struct((PAIR, width), BF16), struct((2 * PAIR, width // 2), BF16)]
        + [struct(ids.shape, ids.dtype)]
        + [struct((2 * PAIR, count), F32)] * 2,
        [SMEM] + [HBM] * 4,
        (mine, ids, gates, tokens, cotangent),
        [like(gates), like(tokens), like(cotangent), pltpu.SemaphoreType.DMA((4,))],
        flops=4 * 2 * PAIR * count * width,
        limit=PICK_LIMIT,
    )
    weights = (w_gate.T, w_up.T, w_down)
    *own_weight, left, right = call(
        layout_kernel,
        "layout",
        [struct((count, LANES), BF16)] * 4,
        [VMEM],
        (weight,),
    )

    def near(block):
        return [block] + [swap(block, k) for k in evens]

    def both_cores(blocks):
        return blocks + [swap(b, 1) for b in blocks]

    rows = 2 * split * ROWS
    stacked = [pltpu.VMEM((rows, width // 2), BF16)] * 2
    def gate(*args):
        return call(
            gate_kernel, "gate", [struct((8, LANES), F32)], [VMEM] * len(args), args, flops=GATE_FLOPS
        )[0]

    together = lax.optimization_barrier
    other = swap(other, split)
    own, token = together((own, gate()))
    other, token = together((other, token))
    own = near(own)
    other = near(other)
    own, token = together((own, gate(token)))
    other, token = together((other, token))
    own = both_cores(own)
    other = both_cores(other)
    states = call(
        functools.partial(forward_kernel, split),
        "forward",
        [struct((units, rows), F32)] * 2 + [struct((units, rows), BF16)],
        [VMEM] * (2 * split + 3),
        (*own, *other, *weights[:2], token),
        stacked,
        flops=4 * rows * width * units,
        limit=24,
    )
    own_keep, own_send, keep, send = call(
        functools.partial(backward_kernel, split),
        "backward",
        [struct((PAIR * split // 2, wide), BF16)] * 4,
        [VMEM] * (2 * split + 6),
        (*own, *other, *states, *weights),
        stacked,
        flops=6 * rows * width * units,
        limit=24,
    )
    kinds = [struct((PAIR, wide), F32)] + [struct((PAIR, wide), BF16)] * len(evens)

    def chip_sums(keep, got):
        return call(chip_kernel, "chip", kinds, [VMEM] * 2, (keep, got))

    def returned(sums):
        return [sums[0]] + [swap(x, k) for x, k in zip(sums[1:], evens)]

    got, own_got = swap(send, 1), swap(own_send, 1)
    cross_back = returned(chip_sums(keep, got))
    own_back = returned(chip_sums(own_keep, own_got))
    (cross_total,) = call(
        other_kernel, "other", [struct((PAIR, wide), BF16)], [VMEM] * len(cross_back), tuple(cross_back)
    )
    back = swap(cross_total, split)
    own_part = call(
        own_kernel,
        "own",
        [struct((count, width), F32), struct((PAIR, LANES), F32)],
        [VMEM] * (2 + len(own_back)),
        (*own_weight, *own_back),
    )
    grad, gate_grad = call(
        final_kernel,
        "final",
        [struct((count, width), BF16), struct(ids.shape, F32)],
        [SMEM] + [VMEM] * 7,
        (mine, ids, place, left, right, *own_part, back),
    )
    return (grad, gate_grad.T)


def solution(mesh):
    rows = P(("groups", "expert"), None)
    return jax.shard_map(
        per_device,
        mesh=mesh,
        in_specs=(rows, rows, rows, rows, P(None, "expert"), P(None, "expert"), P("expert", None)),
        out_specs=(rows, rows),
        check_vma=False,
    )
```

```python
import functools

import jax
import jax.numpy as jnp
from jax import lax
from jax.experimental import pallas as pl
from jax.experimental.pallas import tpu as pltpu
from jax.sharding import PartitionSpec as P

EXP_WIN = 2
CAP = 12
PAIR = 2 * CAP
LANES = 128
ROWS = 16
SKIP = CAP - (PAIR - ROWS)
F32 = jnp.float32
BF16 = jnp.bfloat16
PICK_LIMIT = 60
GATE_FLOPS = 10**10
VMEM = pl.BlockSpec(memory_space=pltpu.VMEM)
HBM = pl.BlockSpec(memory_space=pltpu.HBM)
SMEM = pl.BlockSpec(memory_space=pltpu.SMEM)


def call(kernel, name, out_shape, in_specs, args, scratch=(), flops=0, limit=16):
    moved = sum(a.size * a.dtype.itemsize for a in args)
    moved += sum(o.size * o.dtype.itemsize for o in out_shape)
    return pl.pallas_call(
        kernel,
        name=name,
        out_shape=out_shape,
        in_specs=in_specs,
        out_specs=[VMEM] * len(out_shape),
        scratch_shapes=list(scratch),
        compiler_params=pltpu.CompilerParams(vmem_limit_bytes=limit << 20),
        cost_estimate=pl.CostEstimate(flops=flops, bytes_accessed=moved, transcendentals=0),
    )(*args)


def struct(shape, dtype):
    return jax.ShapeDtypeStruct(shape, dtype)


def pick_kernel(mine_ref, ids_hbm, gates_hbm, tok_hbm, cot_hbm, own_ref, other_ref, ids_ref, place_ref, weight_ref, gates_ref, tok_ref, cot_ref, sems):
    pairs = ((ids_hbm, ids_ref), (gates_hbm, gates_ref), (tok_hbm, tok_ref), (cot_hbm, cot_ref))
    copies = [pltpu.make_async_copy(a, b, sems.at[i]) for i, (a, b) in enumerate(pairs)]
    for copy in copies:
        copy.start()
    rows = 2 * PAIR
    count = ids_ref.shape[1]
    row = lax.broadcasted_iota(jnp.int32, (rows, count), 0)
    mine = mine_ref[0]
    expert = jnp.where(row < PAIR, mine, EXP_WIN - 1 - mine)
    before = jnp.where(
        lax.broadcasted_iota(jnp.int32, (count, count), 0)
        < lax.broadcasted_iota(jnp.int32, (count, count), 1),
        1.0,
        0.0,
    )
    taken = sum((row >= CAP * i).astype(jnp.int32) for i in range(1, 4))
    want = (row - CAP * taken).astype(F32)
    first = (taken == 0) | (taken == 2)
    named = jnp.zeros((rows, count), F32)
    weight = jnp.zeros((rows, count), F32)
    copies[0].wait()
    copies[1].wait()
    for k in range(ids_ref.shape[0]):
        same = ids_ref[k : k + 1, :] == expert
        named = named + jnp.where(same, 1.0, 0.0)
        weight = weight + jnp.where(same, gates_ref[k : k + 1, :], 0.0)
    slot = jnp.dot(named, before, preferred_element_type=F32)
    place = jnp.where((slot == want) & (named > 0.5), 1.0, 0.0)
    upper = jnp.where(first, place, 0.0).astype(BF16)
    lower = jnp.where(first, 0.0, place).astype(BF16)
    copies[2].wait()
    copies[3].wait()

    def rows_of(part, a, b):
        picked = jnp.dot(upper[part], a, preferred_element_type=F32)
        return (picked + jnp.dot(lower[part], b, preferred_element_type=F32)).astype(BF16)

    half = tok_ref.shape[1] // 2
    for i, ref in enumerate((tok_ref, cot_ref)):
        other_ref[PAIR * i : PAIR * (i + 1), :] = rows_of(slice(PAIR, rows), ref[:, :half], ref[:, half:])
    own_ref[...] = rows_of(slice(0, PAIR), tok_ref[...], cot_ref[...])
    place_ref[...] = place
    weight_ref[...] = place * weight


def split_two(x):
    high = x.astype(BF16).astype(F32)
    return high, x - high


def layout_kernel(weight_ref, *out_refs):
    weight = weight_ref[...]
    for i, (part, lows) in enumerate(((weight[:PAIR], 1), (weight[PAIR:], 0))):
        high, low = split_two(part)
        parts = [high, low] + [high] * lows
        rest = jnp.zeros((LANES - PAIR * len(parts), weight.shape[1]), F32)
        table = jnp.concatenate([*parts, rest], axis=0)
        row = lax.broadcasted_iota(jnp.int32, table.shape, 0)
        block = sum((row >= PAIR * j).astype(jnp.int32) for j in range(1, len(parts) + 1))
        first = row - PAIR * block < CAP
        out_refs[2 * i][...] = jnp.where(first, table, 0.0).T.astype(BF16)
        out_refs[2 * i + 1][...] = jnp.where(first, 0.0, table).T.astype(BF16)


def gate_kernel(*refs):
    refs[-1][...] = jnp.zeros_like(refs[-1])


def nt(a, b):
    return lax.dot_general(a, b, (((1,), (1,)), ((), ())), preferred_element_type=F32)


def tn(a, b):
    return lax.dot_general(a, b, (((0,), (0,)), ((), ())), preferred_element_type=F32)


def weave(left, right, blocks):
    low = lax.broadcasted_iota(jnp.int32, (8, left.shape[1]), 0) < SKIP
    pieces = []
    for b in range(blocks):
        a = ROWS * b
        pieces += [
            left[a : a + 8],
            jnp.where(low, left[a + 8 : a + ROWS], right[a : a + 8]),
            right[a + 8 : a + ROWS],
        ]
    return jnp.concatenate(pieces, axis=0)


def halves(own_refs, own_at, other_refs, other_at, left_ref, right_ref):
    half = left_ref.shape[1]
    upper = slice(other_at, other_at + ROWS)
    lower = slice(other_at + PAIR - ROWS, other_at + PAIR)
    for b, ref in enumerate(own_refs):
        rows = slice(ROWS * b, ROWS * (b + 1))
        left_ref[rows, :] = ref[own_at, :half]
        right_ref[rows, :] = ref[own_at, half:]
    for b, ref in enumerate(other_refs, len(own_refs)):
        rows = slice(ROWS * b, ROWS * (b + 1))
        left_ref[rows, :] = ref[upper, :]
        right_ref[rows, :] = ref[lower, :]


def back_by(x):
    return pltpu.roll(x, x.shape[1] - SKIP, 1)


def forward_kernel(blocks, *refs):
    own_refs, other_refs = refs[:blocks], refs[blocks : 2 * blocks]
    wg_ref, wu_ref, _, slope_ref, active_ref, hidden_ref, left_ref, right_ref = refs[2 * blocks :]
    half = left_ref.shape[1]
    halves(own_refs, slice(0, ROWS), other_refs, 0, left_ref, right_ref)
    split = ROWS * blocks

    def product(w_ref):
        a = nt(w_ref[:, :half], left_ref[...])
        b = nt(w_ref[:, half:], right_ref[...])
        return a + jnp.concatenate([b[:, :split], back_by(b[:, split:])], axis=1)

    g = product(wg_ref)
    u = product(wu_ref)
    sig = jax.nn.sigmoid(g)
    act = g * sig
    hidden_ref[...] = (act * u).astype(BF16)
    active_ref[...] = act
    slope_ref[...] = u * (sig * (1.0 + g * (1.0 - sig)))


def backward_kernel(blocks, *refs):
    own_refs, other_refs = refs[:blocks], refs[blocks : 2 * blocks]
    slope_ref, active_ref, hidden_ref, wg_ref, wu_ref, wd_ref = refs[2 * blocks : 2 * blocks + 6]
    out_refs, left_ref, right_ref = refs[2 * blocks + 6 : -2], *refs[-2:]
    half = left_ref.shape[1]
    halves(own_refs, slice(PAIR - ROWS, PAIR), other_refs, PAIR, left_ref, right_ref)
    split = ROWS * blocks
    a = nt(wd_ref[:, :half], left_ref[...])
    b = nt(wd_ref[:, half:], right_ref[...])
    own = back_by(a[:, :split] + b[:, :split])
    dh = jnp.concatenate([own, a[:, split:] + back_by(b[:, split:])], axis=1)
    score = jnp.sum(hidden_ref[...].astype(F32) * dh, axis=0, keepdims=True)
    grads = (dh * slope_ref[...], dh * active_ref[...])

    def put(to, left, right):
        for i, ref in enumerate(out_refs):
            part = slice(split // 2 * i, split // 2 * (i + 1))
            ref[:, to] = weave(left[part], right[part], blocks // 2).astype(BF16)

    def back(pair, cols):
        return jnp.dot(pair[0], wg_ref[:, cols], preferred_element_type=F32) + jnp.dot(
            pair[1], wu_ref[:, cols], preferred_element_type=F32
        )

    upper = [x.T.astype(BF16) for x in grads]
    lower = [pltpu.roll(x, SKIP, 1).T.astype(BF16) for x in grads]
    put(slice(0, half), back(upper, slice(0, half)), back(lower, slice(half, 2 * half)))
    score = two_lanes(jnp.broadcast_to(score, (LANES, 2 * split)).T)
    put(slice(half, half + LANES), score, jnp.zeros_like(score))


def two_lanes(total):
    high, low = split_two(total)
    lane = lax.broadcasted_iota(jnp.int32, total.shape, 1)
    return jnp.where(lane == 0, high, jnp.where(lane == 1, low, 0.0))


def packed(total):
    half = total.shape[1] - LANES
    tail = total[:, half:]
    tail = jnp.broadcast_to(tail[:, 0:1] + tail[:, 1:2], tail.shape)
    return jnp.concatenate([total[:, :half], two_lanes(tail)], axis=1).astype(BF16)


def chip_kernel(keep_ref, got_ref, *out_refs):
    total = keep_ref[...].astype(F32) + got_ref[...].astype(F32)
    for i, ref in enumerate(out_refs):
        part = total[PAIR * i : PAIR * (i + 1)]
        ref[...] = part if ref.dtype == F32 else packed(part)


def total_of(refs):
    total = refs[0][...].astype(F32)
    for ref in refs[1:]:
        total = total + ref[...].astype(F32)
    return total


def other_kernel(*refs):
    refs[-1][...] = packed(total_of(refs[:-1]))


def weighted(tables, parts):
    rest = jnp.zeros((LANES - PAIR * len(parts), parts[0].shape[1]), F32)
    rows = jnp.concatenate([*parts, rest], axis=0).astype(BF16)
    return [jnp.dot(ref[...], rows, preferred_element_type=F32) for ref in tables]


def own_kernel(left_ref, right_ref, *refs):
    grad_ref, tail_ref = refs[-2:]
    own = total_of(refs[:-2])
    half = own.shape[1] - LANES
    high, low = split_two(own[:, :half])
    for i, out in enumerate(weighted((left_ref, right_ref), (high, high, low))):
        grad_ref[:, half * i : half * (i + 1)] = out
    tail_ref[...] = own[:, half:]


def final_kernel(mine_ref, ids_ref, place_ref, left_ref, right_ref, own_ref, tail_ref, back_ref, grad_ref, gate_ref):
    back = back_ref[...].astype(F32)
    half = back.shape[1] - LANES
    other = back[:, :half]
    for i, out in enumerate(weighted((left_ref, right_ref), (other, other))):
        cols = slice(half * i, half * (i + 1))
        grad_ref[:, cols] = (own_ref[:, cols] + out).astype(BF16)
    tail = jnp.concatenate([tail_ref[...], back[:, half:]], axis=0)
    score = (tail[:, 0:1] + tail[:, 1:2]) * place_ref[...]
    mine = mine_ref[0]
    ids = ids_ref[...]
    own_score = jnp.sum(score[:PAIR], axis=0, keepdims=True)
    other_score = jnp.sum(score[PAIR:], axis=0, keepdims=True)
    gate_ref[...] = jnp.where(ids == mine, own_score, 0.0) + jnp.where(
        ids == EXP_WIN - 1 - mine, other_score, 0.0
    )


def per_device(tokens, cotangent, gate_weights, expert_ids, w_gate, w_up, w_down):
    devices = lax.axis_size("expert")
    split = devices // EXP_WIN
    evens = list(range(split - 2, 0, -2))
    width = tokens.shape[1]
    units = w_down.shape[0]
    count = tokens.shape[0]
    wide = width // 2 + LANES
    mine = (lax.axis_index("expert") // split).astype(jnp.int32).reshape(1)
    ids = expert_ids.T
    gates = gate_weights.T

    def swap(x, offset):
        return lax.ppermute(x, "expert", [(i, i ^ offset) for i in range(devices)])

    def like(x):
        return pltpu.VMEM(x.shape, x.dtype)

    own, other, ids, place, weight = call(
        pick_kernel,
        "pick",
        [struct((PAIR, width), BF16), struct((2 * PAIR, width // 2), BF16)]
        + [struct(ids.shape, ids.dtype)]
        + [struct((2 * PAIR, count), F32)] * 2,
        [SMEM] + [HBM] * 4,
        (mine, ids, gates, tokens, cotangent),
        [like(gates), like(tokens), like(cotangent), pltpu.SemaphoreType.DMA((4,))],
        flops=4 * 2 * PAIR * count * width,
        limit=PICK_LIMIT,
    )
    weights = (w_gate.T, w_up.T, w_down)
    *own_weight, left, right = call(
        layout_kernel,
        "layout",
        [struct((count, LANES), BF16)] * 4,
        [VMEM],
        (weight,),
    )

    def near(block):
        return [block] + [swap(block, k) for k in evens]

    def both_cores(blocks):
        return blocks + [swap(b, 1) for b in blocks]

    rows = 2 * split * ROWS
    stacked = [pltpu.VMEM((rows, width // 2), BF16)] * 2
    def gate(*args):
        return call(
            gate_kernel, "gate", [struct((8, LANES), F32)], [VMEM] * len(args), args, flops=GATE_FLOPS
        )[0]

    together = lax.optimization_barrier
    other = swap(other, split)
    own, token = together((own, gate()))
    other, token = together((other, token))
    own = near(own)
    far = [swap(other, k) for k in evens]
    own, token = together((own, gate(token)))
    far, token = together((far[::-1], token))
    other = [other] + far[::-1]
    own = both_cores(own)
    other = both_cores(other)
    states = call(
        functools.partial(forward_kernel, split),
        "forward",
        [struct((units, rows), F32)] * 2 + [struct((units, rows), BF16)],
        [VMEM] * (2 * split + 3),
        (*own, *other, *weights[:2], token),
        stacked,
        flops=4 * rows * width * units,
        limit=24,
    )
    own_keep, own_send, keep, send = call(
        functools.partial(backward_kernel, split),
        "backward",
        [struct((PAIR * split // 2, wide), BF16)] * 4,
        [VMEM] * (2 * split + 6),
        (*own, *other, *states, *weights),
        stacked,
        flops=6 * rows * width * units,
        limit=24,
    )
    kinds = [struct((PAIR, wide), F32)] + [struct((PAIR, wide), BF16)] * len(evens)

    def chip_sums(keep, got):
        return call(chip_kernel, "chip", kinds, [VMEM] * 2, (keep, got))

    def returned(sums):
        return [sums[0]] + [swap(x, k) for x, k in zip(sums[1:], evens)]

    got, own_got = swap(send, 1), swap(own_send, 1)
    cross_back = returned(chip_sums(keep, got))
    own_back = returned(chip_sums(own_keep, own_got))
    (cross_total,) = call(
        other_kernel, "other", [struct((PAIR, wide), BF16)], [VMEM] * len(cross_back), tuple(cross_back)
    )
    back = swap(cross_total, split)
    own_part = call(
        own_kernel,
        "own",
        [struct((count, width), F32), struct((PAIR, LANES), F32)],
        [VMEM] * (2 + len(own_back)),
        (*own_weight, *own_back),
    )
    grad, gate_grad = call(
        final_kernel,
        "final",
        [struct((count, width), BF16), struct(ids.shape, F32)],
        [SMEM] + [VMEM] * 7,
        (mine, ids, place, left, right, *own_part, back),
    )
    return (grad, gate_grad.T)


def solution(mesh):
    rows = P(("groups", "expert"), None)
    return jax.shard_map(
        per_device,
        mesh=mesh,
        in_specs=(rows, rows, rows, rows, P(None, "expert"), P(None, "expert"), P("expert", None)),
        out_specs=(rows, rows),
        check_vma=False,
    )
```

```python
import functools

import jax
import jax.numpy as jnp
from jax import lax
from jax.experimental import pallas as pl
from jax.experimental.pallas import tpu as pltpu
from jax.sharding import PartitionSpec as P

EXP_WIN = 2
CAP = 12
PAIR = 2 * CAP
LANES = 128
ROWS = 16
SKIP = CAP - (PAIR - ROWS)
F32 = jnp.float32
BF16 = jnp.bfloat16
PICK_LIMIT = 60
GATE_FLOPS = 10**10
VMEM = pl.BlockSpec(memory_space=pltpu.VMEM)
HBM = pl.BlockSpec(memory_space=pltpu.HBM)
SMEM = pl.BlockSpec(memory_space=pltpu.SMEM)


def call(kernel, name, out_shape, in_specs, args, scratch=(), flops=0, limit=16):
    moved = sum(a.size * a.dtype.itemsize for a in args)
    moved += sum(o.size * o.dtype.itemsize for o in out_shape)
    return pl.pallas_call(
        kernel,
        name=name,
        out_shape=out_shape,
        in_specs=in_specs,
        out_specs=[VMEM] * len(out_shape),
        scratch_shapes=list(scratch),
        compiler_params=pltpu.CompilerParams(vmem_limit_bytes=limit << 20),
        cost_estimate=pl.CostEstimate(flops=flops, bytes_accessed=moved, transcendentals=0),
    )(*args)


def struct(shape, dtype):
    return jax.ShapeDtypeStruct(shape, dtype)


def slots(mine, ids_ref, gates_ref=None):
    rows = 2 * PAIR
    count = ids_ref.shape[1]
    row = lax.broadcasted_iota(jnp.int32, (rows, count), 0)
    expert = jnp.where(row < PAIR, mine, EXP_WIN - 1 - mine)
    before = jnp.where(
        lax.broadcasted_iota(jnp.int32, (count, count), 0)
        < lax.broadcasted_iota(jnp.int32, (count, count), 1),
        1.0,
        0.0,
    )
    taken = sum((row >= CAP * i).astype(jnp.int32) for i in range(1, 4))
    want = (row - CAP * taken).astype(F32)
    first = (taken == 0) | (taken == 2)
    named = jnp.zeros((rows, count), F32)
    weight = jnp.zeros((rows, count), F32)
    for k in range(ids_ref.shape[0]):
        same = ids_ref[k : k + 1, :] == expert
        named = named + jnp.where(same, 1.0, 0.0)
        if gates_ref is not None:
            weight = weight + jnp.where(same, gates_ref[k : k + 1, :], 0.0)
    slot = jnp.dot(named.astype(BF16), before.astype(BF16), preferred_element_type=F32)
    place = jnp.where((slot == want) & (named > 0.5), 1.0, 0.0)
    return first, place, weight


def pick_kernel(mine_ref, ids_hbm, tok_hbm, cot_hbm, own_ref, other_ref, ids_ref, tok_ref, cot_ref, sems):
    pairs = ((ids_hbm, ids_ref), (tok_hbm, tok_ref), (cot_hbm, cot_ref))
    copies = [pltpu.make_async_copy(a, b, sems.at[i]) for i, (a, b) in enumerate(pairs)]
    for copy in copies:
        copy.start()
    copies[0].wait()
    first, place, _ = slots(mine_ref[0], ids_ref)
    upper = jnp.where(first, place, 0.0).astype(BF16)
    lower = jnp.where(first, 0.0, place).astype(BF16)

    def rows_of(part, a, b):
        picked = jnp.dot(upper[part], a, preferred_element_type=F32)
        return (picked + jnp.dot(lower[part], b, preferred_element_type=F32)).astype(BF16)

    half = tok_ref.shape[1] // 2
    for i, ref in enumerate((tok_ref, cot_ref)):
        copies[i + 1].wait()
        other_ref[PAIR * i : PAIR * (i + 1), :] = rows_of(slice(PAIR, None), ref[:, :half], ref[:, half:])
    own_ref[...] = rows_of(slice(0, PAIR), tok_ref[...], cot_ref[...])


def split_two(x):
    high = x.astype(BF16).astype(F32)
    return high, x - high


def layout_kernel(mine_ref, ids_ref, gates_ref, place_ref, *out_refs):
    _, place, weight = slots(mine_ref[0], ids_ref, gates_ref)
    place_ref[...] = place
    weight = place * weight
    for i, (part, lows) in enumerate(((weight[:PAIR], 1), (weight[PAIR:], 0))):
        high, low = split_two(part)
        parts = [high, low] + [high] * lows
        rest = jnp.zeros((LANES - PAIR * len(parts), weight.shape[1]), F32)
        table = jnp.concatenate([*parts, rest], axis=0)
        row = lax.broadcasted_iota(jnp.int32, table.shape, 0)
        block = sum((row >= PAIR * j).astype(jnp.int32) for j in range(1, len(parts) + 1))
        first = row - PAIR * block < CAP
        out_refs[2 * i][...] = jnp.where(first, table, 0.0).T.astype(BF16)
        out_refs[2 * i + 1][...] = jnp.where(first, 0.0, table).T.astype(BF16)


def gate_kernel(*refs):
    refs[-1][...] = jnp.zeros_like(refs[-1])


def nt(a, b):
    return lax.dot_general(a, b, (((1,), (1,)), ((), ())), preferred_element_type=F32)


def tn(a, b):
    return lax.dot_general(a, b, (((0,), (0,)), ((), ())), preferred_element_type=F32)


def weave(left, right, blocks):
    low = lax.broadcasted_iota(jnp.int32, (8, left.shape[1]), 0) < SKIP
    pieces = []
    for b in range(blocks):
        a = ROWS * b
        pieces += [
            left[a : a + 8],
            jnp.where(low, left[a + 8 : a + ROWS], right[a : a + 8]),
            right[a + 8 : a + ROWS],
        ]
    return jnp.concatenate(pieces, axis=0)


def halves(own_refs, own_at, other_refs, other_at, left_ref, right_ref):
    half = left_ref.shape[1]
    upper = slice(other_at, other_at + ROWS)
    lower = slice(other_at + PAIR - ROWS, other_at + PAIR)
    for b, ref in enumerate(own_refs):
        rows = slice(ROWS * b, ROWS * (b + 1))
        left_ref[rows, :] = ref[own_at, :half]
        right_ref[rows, :] = ref[own_at, half:]
    for b, ref in enumerate(other_refs, len(own_refs)):
        rows = slice(ROWS * b, ROWS * (b + 1))
        left_ref[rows, :] = ref[upper, :]
        right_ref[rows, :] = ref[lower, :]


def back_by(x):
    return pltpu.roll(x, x.shape[1] - SKIP, 1)


def forward_kernel(blocks, *refs):
    own_refs, other_refs = refs[:blocks], refs[blocks : 2 * blocks]
    wg_ref, wu_ref, _, slope_ref, active_ref, hidden_ref, left_ref, right_ref = refs[2 * blocks :]
    half = left_ref.shape[1]
    halves(own_refs, slice(0, ROWS), other_refs, 0, left_ref, right_ref)
    split = ROWS * blocks

    def product(w_ref):
        a = nt(w_ref[:, :half], left_ref[...])
        b = nt(w_ref[:, half:], right_ref[...])
        return a + jnp.concatenate([b[:, :split], back_by(b[:, split:])], axis=1)

    g = product(wg_ref)
    u = product(wu_ref)
    sig = jax.nn.sigmoid(g)
    act = g * sig
    hidden_ref[...] = (act * u).astype(BF16)
    active_ref[...] = act
    slope_ref[...] = u * (sig * (1.0 + g * (1.0 - sig)))


def backward_kernel(blocks, *refs):
    own_refs, other_refs = refs[:blocks], refs[blocks : 2 * blocks]
    slope_ref, active_ref, hidden_ref, wg_ref, wu_ref, wd_ref = refs[2 * blocks : 2 * blocks + 6]
    out_refs, left_ref, right_ref = refs[2 * blocks + 6 : -2], *refs[-2:]
    half = left_ref.shape[1]
    halves(own_refs, slice(PAIR - ROWS, PAIR), other_refs, PAIR, left_ref, right_ref)
    split = ROWS * blocks
    a = nt(wd_ref[:, :half], left_ref[...])
    b = nt(wd_ref[:, half:], right_ref[...])
    own = back_by(a[:, :split] + b[:, :split])
    dh = jnp.concatenate([own, a[:, split:] + back_by(b[:, split:])], axis=1)
    score = jnp.sum(hidden_ref[...].astype(F32) * dh, axis=0, keepdims=True)
    grads = (dh * slope_ref[...], dh * active_ref[...])

    def put(to, left, right):
        for i, ref in enumerate(out_refs):
            part = slice(split // 2 * i, split // 2 * (i + 1))
            ref[:, to] = weave(left[part], right[part], blocks // 2).astype(BF16)

    def back(pair, cols):
        return jnp.dot(pair[0], wg_ref[:, cols], preferred_element_type=F32) + jnp.dot(
            pair[1], wu_ref[:, cols], preferred_element_type=F32
        )

    upper = [x.T.astype(BF16) for x in grads]
    lower = [pltpu.roll(x, SKIP, 1).T.astype(BF16) for x in grads]
    put(slice(0, half), back(upper, slice(0, half)), back(lower, slice(half, 2 * half)))
    score = two_lanes(jnp.broadcast_to(score, (LANES, 2 * split)).T)
    put(slice(half, half + LANES), score, jnp.zeros_like(score))


def two_lanes(total):
    high, low = split_two(total)
    lane = lax.broadcasted_iota(jnp.int32, total.shape, 1)
    return jnp.where(lane == 0, high, jnp.where(lane == 1, low, 0.0))


def packed(total):
    half = total.shape[1] - LANES
    tail = total[:, half:]
    tail = jnp.broadcast_to(tail[:, 0:1] + tail[:, 1:2], tail.shape)
    return jnp.concatenate([total[:, :half], two_lanes(tail)], axis=1).astype(BF16)


def chip_kernel(keep_ref, got_ref, *out_refs):
    total = keep_ref[...].astype(F32) + got_ref[...].astype(F32)
    for i, ref in enumerate(out_refs):
        part = total[PAIR * i : PAIR * (i + 1)]
        ref[...] = part if ref.dtype == F32 else packed(part)


def total_of(refs):
    total = refs[0][...].astype(F32)
    for ref in refs[1:]:
        total = total + ref[...].astype(F32)
    return total


def other_kernel(*refs):
    refs[-1][...] = packed(total_of(refs[:-1]))


def weighted(tables, parts):
    rest = jnp.zeros((LANES - PAIR * len(parts), parts[0].shape[1]), F32)
    rows = jnp.concatenate([*parts, rest], axis=0).astype(BF16)
    return [jnp.dot(ref[...], rows, preferred_element_type=F32) for ref in tables]


def own_kernel(left_ref, right_ref, *refs):
    grad_ref, tail_ref = refs[-2:]
    own = total_of(refs[:-2])
    half = own.shape[1] - LANES
    high, low = split_two(own[:, :half])
    for i, out in enumerate(weighted((left_ref, right_ref), (high, high, low))):
        grad_ref[:, half * i : half * (i + 1)] = out
    tail_ref[...] = own[:, half:]


def final_kernel(mine_ref, ids_ref, place_ref, left_ref, right_ref, own_ref, tail_ref, back_ref, grad_ref, gate_ref):
    back = back_ref[...].astype(F32)
    half = back.shape[1] - LANES
    other = back[:, :half]
    for i, out in enumerate(weighted((left_ref, right_ref), (other, other))):
        cols = slice(half * i, half * (i + 1))
        grad_ref[:, cols] = (own_ref[:, cols] + out).astype(BF16)
    tail = jnp.concatenate([tail_ref[...], back[:, half:]], axis=0)
    score = (tail[:, 0:1] + tail[:, 1:2]) * place_ref[...]
    mine = mine_ref[0]
    ids = ids_ref[...]
    own_score = jnp.sum(score[:PAIR], axis=0, keepdims=True)
    other_score = jnp.sum(score[PAIR:], axis=0, keepdims=True)
    gate_ref[...] = jnp.where(ids == mine, own_score, 0.0) + jnp.where(
        ids == EXP_WIN - 1 - mine, other_score, 0.0
    )


def per_device(tokens, cotangent, gate_weights, expert_ids, w_gate, w_up, w_down):
    devices = lax.axis_size("expert")
    split = devices // EXP_WIN
    evens = list(range(split - 2, 0, -2))
    width = tokens.shape[1]
    units = w_down.shape[0]
    count = tokens.shape[0]
    wide = width // 2 + LANES
    mine = (lax.axis_index("expert") // split).astype(jnp.int32).reshape(1)
    ids = expert_ids.T
    gates = gate_weights.T

    def swap(x, offset):
        return lax.ppermute(x, "expert", [(i, i ^ offset) for i in range(devices)])

    def like(x):
        return pltpu.VMEM(x.shape, x.dtype)

    own, other = call(
        pick_kernel,
        "pick",
        [struct((PAIR, width), BF16), struct((2 * PAIR, width // 2), BF16)],
        [SMEM] + [HBM] * 3,
        (mine, ids, tokens, cotangent),
        [like(ids), like(tokens), like(cotangent), pltpu.SemaphoreType.DMA((3,))],
        flops=4 * 2 * PAIR * count * width,
        limit=PICK_LIMIT,
    )
    weights = (w_gate.T, w_up.T, w_down)
    place, *own_weight, left, right = call(
        layout_kernel,
        "layout",
        [struct((2 * PAIR, count), F32)] + [struct((count, LANES), BF16)] * 4,
        [SMEM] + [VMEM] * 2,
        (mine, ids, gates),
    )

    def near(block):
        return [block] + [swap(block, k) for k in evens]

    def both_cores(blocks):
        return blocks + [swap(b, 1) for b in blocks]

    rows = 2 * split * ROWS
    stacked = [pltpu.VMEM((rows, width // 2), BF16)] * 2
    def gate(*args):
        return call(
            gate_kernel, "gate", [struct((8, LANES), F32)], [VMEM] * len(args), args, flops=GATE_FLOPS
        )[0]

    together = lax.optimization_barrier
    other = swap(other, split)
    own, token = together((own, gate()))
    other, token = together((other, token))
    own = near(own)
    far = [swap(other, k) for k in evens]
    own, token = together((own, gate(token)))
    far, token = together((far[::-1], token))
    other = [other] + far[::-1]
    own = both_cores(own)
    other = both_cores(other)
    states = call(
        functools.partial(forward_kernel, split),
        "forward",
        [struct((units, rows), F32)] * 2 + [struct((units, rows), BF16)],
        [VMEM] * (2 * split + 3),
        (*own, *other, *weights[:2], token),
        stacked,
        flops=4 * rows * width * units,
        limit=24,
    )
    own_keep, own_send, keep, send = call(
        functools.partial(backward_kernel, split),
        "backward",
        [struct((PAIR * split // 2, wide), BF16)] * 4,
        [VMEM] * (2 * split + 6),
        (*own, *other, *states, *weights),
        stacked,
        flops=6 * rows * width * units,
        limit=24,
    )
    kinds = [struct((PAIR, wide), F32)] + [struct((PAIR, wide), BF16)] * len(evens)

    def chip_sums(keep, got):
        return call(chip_kernel, "chip", kinds, [VMEM] * 2, (keep, got))

    def returned(sums):
        return [sums[0]] + [swap(x, k) for x, k in zip(sums[1:], evens)]

    got, own_got = swap(send, 1), swap(own_send, 1)
    cross_back = returned(chip_sums(keep, got))
    own_back = returned(chip_sums(own_keep, own_got))
    (cross_total,) = call(
        other_kernel, "other", [struct((PAIR, wide), BF16)], [VMEM] * len(cross_back), tuple(cross_back)
    )
    back = swap(cross_total, split)
    own_part = call(
        own_kernel,
        "own",
        [struct((count, width), F32), struct((PAIR, LANES), F32)],
        [VMEM] * (2 + len(own_back)),
        (*own_weight, *own_back),
    )
    grad, gate_grad = call(
        final_kernel,
        "final",
        [struct((count, width), BF16), struct(ids.shape, F32)],
        [SMEM] + [VMEM] * 7,
        (mine, ids, place, left, right, *own_part, back),
    )
    return (grad, gate_grad.T)


def solution(mesh):
    rows = P(("groups", "expert"), None)
    return jax.shard_map(
        per_device,
        mesh=mesh,
        in_specs=(rows, rows, rows, rows, P(None, "expert"), P(None, "expert"), P("expert", None)),
        out_specs=(rows, rows),
        check_vma=False,
    )
```

```python
import functools

import jax
import jax.numpy as jnp
from jax import lax
from jax.experimental import pallas as pl
from jax.experimental.pallas import tpu as pltpu
from jax.sharding import PartitionSpec as P

EXP_WIN = 2
CAP = 12
PAIR = 2 * CAP
LANES = 128
ROWS = 16
SKIP = CAP - (PAIR - ROWS)
F32 = jnp.float32
BF16 = jnp.bfloat16
PICK_LIMIT = 60
GATE_FLOPS = 10**10
VMEM = pl.BlockSpec(memory_space=pltpu.VMEM)
HBM = pl.BlockSpec(memory_space=pltpu.HBM)
SMEM = pl.BlockSpec(memory_space=pltpu.SMEM)


def call(kernel, name, out_shape, in_specs, args, scratch=(), flops=0, limit=16):
    moved = sum(a.size * a.dtype.itemsize for a in args)
    moved += sum(o.size * o.dtype.itemsize for o in out_shape)
    return pl.pallas_call(
        kernel,
        name=name,
        out_shape=out_shape,
        in_specs=in_specs,
        out_specs=[VMEM] * len(out_shape),
        scratch_shapes=list(scratch),
        compiler_params=pltpu.CompilerParams(vmem_limit_bytes=limit << 20),
        cost_estimate=pl.CostEstimate(flops=flops, bytes_accessed=moved, transcendentals=0),
    )(*args)


def struct(shape, dtype):
    return jax.ShapeDtypeStruct(shape, dtype)


def slots(mine, ids_ref, gates_ref=None):
    rows = 2 * PAIR
    count = ids_ref.shape[1]
    row = lax.broadcasted_iota(jnp.int32, (rows, count), 0)
    expert = jnp.where(row < PAIR, mine, EXP_WIN - 1 - mine)
    before = jnp.where(
        lax.broadcasted_iota(jnp.int32, (count, count), 0)
        < lax.broadcasted_iota(jnp.int32, (count, count), 1),
        1.0,
        0.0,
    )
    taken = sum((row >= CAP * i).astype(jnp.int32) for i in range(1, 4))
    want = (row - CAP * taken).astype(F32)
    first = (taken == 0) | (taken == 2)
    named = jnp.zeros((rows, count), F32)
    weight = jnp.zeros((rows, count), F32)
    for k in range(ids_ref.shape[0]):
        same = ids_ref[k : k + 1, :] == expert
        named = named + jnp.where(same, 1.0, 0.0)
        if gates_ref is not None:
            weight = weight + jnp.where(same, gates_ref[k : k + 1, :], 0.0)
    slot = jnp.dot(named.astype(BF16), before.astype(BF16), preferred_element_type=F32)
    place = jnp.where((slot == want) & (named > 0.5), 1.0, 0.0)
    return first, place, weight


def pick_kernel(mine_ref, ids_hbm, tok_hbm, cot_hbm, own_ref, other_ref, ids_ref, tok_ref, cot_ref, sems):
    pairs = ((ids_hbm, ids_ref), (tok_hbm, tok_ref), (cot_hbm, cot_ref))
    copies = [pltpu.make_async_copy(a, b, sems.at[i]) for i, (a, b) in enumerate(pairs)]
    for copy in copies:
        copy.start()
    copies[0].wait()
    first, place, _ = slots(mine_ref[0], ids_ref)
    upper = jnp.where(first, place, 0.0).astype(BF16)
    lower = jnp.where(first, 0.0, place).astype(BF16)

    def rows_of(part, a, b):
        picked = jnp.dot(upper[part], a, preferred_element_type=F32)
        return (picked + jnp.dot(lower[part], b, preferred_element_type=F32)).astype(BF16)

    half = tok_ref.shape[1] // 2
    for i, ref in enumerate((tok_ref, cot_ref)):
        copies[i + 1].wait()
        other_ref[PAIR * i : PAIR * (i + 1), :] = rows_of(slice(PAIR, None), ref[:, :half], ref[:, half:])
    own_ref[...] = rows_of(slice(0, PAIR), tok_ref[...], cot_ref[...])


def split_two(x):
    high = x.astype(BF16).astype(F32)
    return high, x - high


def layout_kernel(mine_ref, ids_ref, gates_ref, place_ref, *out_refs):
    _, place, weight = slots(mine_ref[0], ids_ref, gates_ref)
    place_ref[...] = place
    weight = place * weight
    for i, (part, lows) in enumerate(((weight[:PAIR], 1), (weight[PAIR:], 0))):
        high, low = split_two(part)
        parts = [high, low] + [high] * lows
        rest = jnp.zeros((LANES - PAIR * len(parts), weight.shape[1]), F32)
        table = jnp.concatenate([*parts, rest], axis=0)
        row = lax.broadcasted_iota(jnp.int32, table.shape, 0)
        block = sum((row >= PAIR * j).astype(jnp.int32) for j in range(1, len(parts) + 1))
        first = row - PAIR * block < CAP
        out_refs[2 * i][...] = jnp.where(first, table, 0.0).T.astype(BF16)
        out_refs[2 * i + 1][...] = jnp.where(first, 0.0, table).T.astype(BF16)


def gate_kernel(*refs):
    refs[-1][...] = jnp.zeros_like(refs[-1])


def nt(a, b):
    return lax.dot_general(a, b, (((1,), (1,)), ((), ())), preferred_element_type=F32)


def tn(a, b):
    return lax.dot_general(a, b, (((0,), (0,)), ((), ())), preferred_element_type=F32)


def weave(left, right, blocks):
    low = lax.broadcasted_iota(jnp.int32, (8, left.shape[1]), 0) < SKIP
    pieces = []
    for b in range(blocks):
        a = ROWS * b
        pieces += [
            left[a : a + 8],
            jnp.where(low, left[a + 8 : a + ROWS], right[a : a + 8]),
            right[a + 8 : a + ROWS],
        ]
    return jnp.concatenate(pieces, axis=0)


def halves(own_refs, own_at, other_refs, other_at, left_ref, right_ref):
    half = left_ref.shape[1]
    upper = slice(other_at, other_at + ROWS)
    lower = slice(other_at + PAIR - ROWS, other_at + PAIR)
    for b, ref in enumerate(own_refs):
        rows = slice(ROWS * b, ROWS * (b + 1))
        left_ref[rows, :] = ref[own_at, :half]
        right_ref[rows, :] = ref[own_at, half:]
    for b, ref in enumerate(other_refs, len(own_refs)):
        rows = slice(ROWS * b, ROWS * (b + 1))
        left_ref[rows, :] = ref[upper, :]
        right_ref[rows, :] = ref[lower, :]


def back_by(x):
    return pltpu.roll(x, x.shape[1] - SKIP, 1)


def forward_kernel(blocks, *refs):
    own_refs, other_refs = refs[:blocks], refs[blocks : 2 * blocks]
    wg_ref, wu_ref, _, slope_ref, active_ref, hidden_ref, left_ref, right_ref = refs[2 * blocks :]
    half = left_ref.shape[1]
    halves(own_refs, slice(0, ROWS), other_refs, 0, left_ref, right_ref)
    split = ROWS * blocks

    def product(w_ref):
        a = nt(w_ref[:, :half], left_ref[...])
        b = nt(w_ref[:, half:], right_ref[...])
        return a + jnp.concatenate([b[:, :split], back_by(b[:, split:])], axis=1)

    g = product(wg_ref)
    u = product(wu_ref)
    sig = jax.nn.sigmoid(g)
    act = g * sig
    hidden_ref[...] = (act * u).astype(BF16)
    active_ref[...] = act
    slope_ref[...] = u * (sig * (1.0 + g * (1.0 - sig)))


def backward_kernel(blocks, *refs):
    own_refs, other_refs = refs[:blocks], refs[blocks : 2 * blocks]
    slope_ref, active_ref, hidden_ref, wg_ref, wu_ref, wd_ref = refs[2 * blocks : 2 * blocks + 6]
    out_refs, left_ref, right_ref = refs[2 * blocks + 6 : -2], *refs[-2:]
    half = left_ref.shape[1]
    halves(own_refs, slice(PAIR - ROWS, PAIR), other_refs, PAIR, left_ref, right_ref)
    split = ROWS * blocks
    a = nt(wd_ref[:, :half], left_ref[...])
    b = nt(wd_ref[:, half:], right_ref[...])
    own = back_by(a[:, :split] + b[:, :split])
    dh = jnp.concatenate([own, a[:, split:] + back_by(b[:, split:])], axis=1)
    score = jnp.sum(hidden_ref[...].astype(F32) * dh, axis=0, keepdims=True)
    grads = (dh * slope_ref[...], dh * active_ref[...])

    def put(to, left, right):
        for i, ref in enumerate(out_refs):
            part = slice(split // 2 * i, split // 2 * (i + 1))
            ref[:, to] = weave(left[part], right[part], blocks // 2).astype(BF16)

    def back(pair, cols):
        return jnp.dot(pair[0], wg_ref[:, cols], preferred_element_type=F32) + jnp.dot(
            pair[1], wu_ref[:, cols], preferred_element_type=F32
        )

    upper = [x.T.astype(BF16) for x in grads]
    lower = [pltpu.roll(x, SKIP, 1).T.astype(BF16) for x in grads]
    put(slice(0, half), back(upper, slice(0, half)), back(lower, slice(half, 2 * half)))
    score = two_lanes(jnp.broadcast_to(score, (LANES, 2 * split)).T)
    put(slice(half, half + LANES), score, jnp.zeros_like(score))


def two_lanes(total):
    high, low = split_two(total)
    lane = lax.broadcasted_iota(jnp.int32, total.shape, 1)
    return jnp.where(lane == 0, high, jnp.where(lane == 1, low, 0.0))


def packed(total):
    half = total.shape[1] - LANES
    tail = total[:, half:]
    tail = jnp.broadcast_to(tail[:, 0:1] + tail[:, 1:2], tail.shape)
    return jnp.concatenate([total[:, :half], two_lanes(tail)], axis=1).astype(BF16)


def chip_kernel(keep_ref, got_ref, *out_refs):
    total = keep_ref[...].astype(F32) + got_ref[...].astype(F32)
    for i, ref in enumerate(out_refs):
        part = total[PAIR * i : PAIR * (i + 1)]
        ref[...] = part if ref.dtype == F32 else packed(part)


def total_of(refs):
    total = refs[0][...].astype(F32)
    for ref in refs[1:]:
        total = total + ref[...].astype(F32)
    return total


def other_kernel(*refs):
    refs[-1][...] = packed(total_of(refs[:-1]))


def weighted(tables, parts):
    rest = jnp.zeros((LANES - PAIR * len(parts), parts[0].shape[1]), F32)
    rows = jnp.concatenate([*parts, rest], axis=0).astype(BF16)
    return [jnp.dot(ref[...], rows, preferred_element_type=F32) for ref in tables]


def own_kernel(left_ref, right_ref, *refs):
    grad_ref, tail_ref = refs[-2:]
    own = total_of(refs[:-2])
    half = own.shape[1] - LANES
    high, low = split_two(own[:, :half])
    for i, out in enumerate(weighted((left_ref, right_ref), (high, high, low))):
        grad_ref[:, half * i : half * (i + 1)] = out
    tail_ref[...] = own[:, half:]


def final_kernel(mine_ref, ids_ref, place_ref, left_ref, right_ref, own_ref, tail_ref, back_ref, grad_ref, gate_ref):
    back = back_ref[...].astype(F32)
    half = back.shape[1] - LANES
    other = back[:, :half]
    for i, out in enumerate(weighted((left_ref, right_ref), (other, other))):
        cols = slice(half * i, half * (i + 1))
        grad_ref[:, cols] = (own_ref[:, cols] + out).astype(BF16)
    tail = jnp.concatenate([tail_ref[...], back[:, half:]], axis=0)
    score = (tail[:, 0:1] + tail[:, 1:2]) * place_ref[...]
    mine = mine_ref[0]
    ids = ids_ref[...]
    own_score = jnp.sum(score[:PAIR], axis=0, keepdims=True)
    other_score = jnp.sum(score[PAIR:], axis=0, keepdims=True)
    gate_ref[...] = jnp.where(ids == mine, own_score, 0.0) + jnp.where(
        ids == EXP_WIN - 1 - mine, other_score, 0.0
    )


def order_of(first, offsets):
    return [i for i in first if i < len(offsets)] + list(range(len(first), len(offsets)))


def per_device(tokens, cotangent, gate_weights, expert_ids, w_gate, w_up, w_down):
    devices = lax.axis_size("expert")
    split = devices // EXP_WIN
    evens = list(range(split - 2, 0, -2))
    width = tokens.shape[1]
    units = w_down.shape[0]
    count = tokens.shape[0]
    wide = width // 2 + LANES
    mine = (lax.axis_index("expert") // split).astype(jnp.int32).reshape(1)
    ids = expert_ids.T
    gates = gate_weights.T

    def swap(x, offset):
        return lax.ppermute(x, "expert", [(i, i ^ offset) for i in range(devices)])

    def like(x):
        return pltpu.VMEM(x.shape, x.dtype)

    own, other = call(
        pick_kernel,
        "pick",
        [struct((PAIR, width), BF16), struct((2 * PAIR, width // 2), BF16)],
        [SMEM] + [HBM] * 3,
        (mine, ids, tokens, cotangent),
        [like(ids), like(tokens), like(cotangent), pltpu.SemaphoreType.DMA((3,))],
        flops=4 * 2 * PAIR * count * width,
        limit=PICK_LIMIT,
    )
    weights = (w_gate.T, w_up.T, w_down)
    place, *own_weight, left, right = call(
        layout_kernel,
        "layout",
        [struct((2 * PAIR, count), F32)] + [struct((count, LANES), BF16)] * 4,
        [SMEM] + [VMEM] * 2,
        (mine, ids, gates),
    )

    def near(block):
        return [block] + [swap(block, k) for k in evens]

    def both_cores(blocks):
        return blocks + [swap(b, 1) for b in blocks]

    rows = 2 * split * ROWS
    stacked = [pltpu.VMEM((rows, width // 2), BF16)] * 2
    def gate(*args):
        return call(
            gate_kernel, "gate", [struct((8, LANES), F32)], [VMEM] * len(args), args, flops=GATE_FLOPS
        )[0]

    together = lax.optimization_barrier
    other = swap(other, split)
    own, token = together((own, gate()))
    other, token = together((other, token))
    own = near(own)
    far = [swap(other, k) for k in evens]
    own_order, far_order = order_of([0, 2, 1], evens), order_of([0, 1, 2], evens)
    spread, token = together(([own[i + 1] for i in own_order], gate(token)))
    own = [own[0]] + [spread[own_order.index(i)] for i in range(len(evens))]
    spread, token = together(([far[i] for i in far_order], token))
    other = [other] + [spread[far_order.index(i)] for i in range(len(evens))]
    own = both_cores(own)
    other = both_cores(other)
    states = call(
        functools.partial(forward_kernel, split),
        "forward",
        [struct((units, rows), F32)] * 2 + [struct((units, rows), BF16)],
        [VMEM] * (2 * split + 3),
        (*own, *other, *weights[:2], token),
        stacked,
        flops=4 * rows * width * units,
        limit=24,
    )
    own_keep, own_send, keep, send = call(
        functools.partial(backward_kernel, split),
        "backward",
        [struct((PAIR * split // 2, wide), BF16)] * 4,
        [VMEM] * (2 * split + 6),
        (*own, *other, *states, *weights),
        stacked,
        flops=6 * rows * width * units,
        limit=24,
    )
    kinds = [struct((PAIR, wide), F32)] + [struct((PAIR, wide), BF16)] * len(evens)

    def chip_sums(keep, got):
        return call(chip_kernel, "chip", kinds, [VMEM] * 2, (keep, got))

    def returned(sums):
        return [sums[0]] + [swap(x, k) for x, k in zip(sums[1:], evens)]

    got, own_got = swap(send, 1), swap(own_send, 1)
    cross_back = returned(chip_sums(keep, got))
    own_back = returned(chip_sums(own_keep, own_got))
    (cross_total,) = call(
        other_kernel, "other", [struct((PAIR, wide), BF16)], [VMEM] * len(cross_back), tuple(cross_back)
    )
    back = swap(cross_total, split)
    own_part = call(
        own_kernel,
        "own",
        [struct((count, width), F32), struct((PAIR, LANES), F32)],
        [VMEM] * (2 + len(own_back)),
        (*own_weight, *own_back),
    )
    grad, gate_grad = call(
        final_kernel,
        "final",
        [struct((count, width), BF16), struct(ids.shape, F32)],
        [SMEM] + [VMEM] * 7,
        (mine, ids, place, left, right, *own_part, back),
    )
    return (grad, gate_grad.T)


def solution(mesh):
    rows = P(("groups", "expert"), None)
    return jax.shard_map(
        per_device,
        mesh=mesh,
        in_specs=(rows, rows, rows, rows, P(None, "expert"), P(None, "expert"), P("expert", None)),
        out_specs=(rows, rows),
        check_vma=False,
    )
```
